128 devices in a mesh: stn: 16 (over y_lo, z, core), chan: 8 (over x, y_hi).
Axes of the slice: x: 4, y: 4 (y_hi: 2, y_lo: 2; y = y_hi * 2 + y_lo), z: 4, core: 2. Of those that a mesh axis runs over, the one named last changes fastest.
Arguments:
- voltages: bfloat16 [2, 1024, 253952], P(None, ('stn', 'chan')), may hold values from -6 to 6
- filter_taps: float32 [16, 8192], replicated, may hold values from -1.5 to 1.5
- station_flags: int32 [512], P(('stn', 'chan')), may hold values 0 or 1
- subband_lists: int32 [8, 16], replicated, may hold values from 0 to 2047, as said below
- subband_counts: int32 [8], replicated, may hold values from 1 to 16, as said below
Outputs:
- visibilities: float32 [16, 9, 512, 64, 128], P('stn', None, 'chan')
The draws below stay inside these ranges and needn't reach their ends.
Inputs may be any that keep to these rules, and one draw needn't show every extreme that they name: `subband_lists`: each entry names a subband of 4 channels; all 8 x 16 entries differ. Group g uses the subbands of its first subband_counts[g] slots; the other slots are not used.
All inputs are finite; a program needn't handle non-finite values. No bound on the sum of `station_flags` on one device may be relied on, other than what follows from the above.
Results may differ from the reference program's by a relative error of at most 0.0083.
Values may be sent and summed in bfloat16 or wider, within the bound.
No kernel may reach another device: no remote copies, remote signals or barrier semaphores. Data moves between devices by JAX's collectives and lax.ppermute only.
A program may use at most 192 MiB of HBM per device.

```python
import math
import jax
import jax.numpy as jnp
from jax import lax

STATIONS = 512
NCH = 8192
FIRST = 64
SECOND = 128
TAPS = 16
SPECTRA = 16
SUBW = 4
CAP = 16
NSUB = 2048
CAPCH = 64
CHSEL = 512
INPUTS = 1024
INB = 64
NDIST = 9
SAMPLES = 253952
N_STN = 16
N_CHAN = 8


def draw_subband_lists(key, part):
    middle_ids = jax.random.permutation(key, NSUB - 2)[:N_CHAN * CAP - 2].astype(jnp.int32) + 1
    ends = jnp.array([0, NSUB - 1], dtype=jnp.int32)
    chosen = jnp.concatenate([ends, middle_ids])
    shuffled = jax.random.permutation(jax.random.fold_in(key, 7), chosen)
    return shuffled.reshape(N_CHAN, CAP).astype(jnp.int32)


def draw_subband_counts(key, part):
    counted = jax.random.randint(key, (N_CHAN,), 1, CAP // 2 + 1).astype(jnp.int32)
    order = jax.random.permutation(jax.random.fold_in(key, 3), N_CHAN)
    counted = counted.at[order[0]].set(CAP).at[order[1]].set(1)
    return counted.astype(jnp.int32)


def set_ends(entries, stream_key, least, high):
    spot = [jax.random.randint(jax.random.fold_in(stream_key, axis), (), 0, length) for axis, length in enumerate(entries.shape)]
    longest = entries.shape.index(max(entries.shape))
    neighbour = spot[:longest] + [(spot[longest] + 1) % entries.shape[longest]] + spot[longest + 1:]
    return entries.at[tuple(spot)].set(least).at[tuple(neighbour)].set(high)


def shard_levels(key, dims, split, least, largest):
    loudness = 1.0
    for axis_at, blocks in split:
        draws = jax.random.uniform(jax.random.fold_in(jax.random.fold_in(key, 6), axis_at), (blocks,), jnp.float32, least / len(split), largest / len(split))
        loudness = loudness * jnp.repeat(jnp.exp(draws), dims[axis_at] // blocks).reshape((-1,) + (1,) * (len(dims) - 1 - axis_at))
    return loudness


def normal_values(key, dims, width, bound, cuts=(), kind=jnp.bfloat16):
    values = jax.random.normal(key, dims, jnp.float32) * width
    if len(cuts) > 0:
        values = shard_levels(key, dims, cuts, -0.22, 0.18) * values
    return jnp.clip(values, min=-bound, max=bound).astype(kind)


def setup_inputs(seed: int = 0) -> dict:
    key_of = jax.random.split(jax.random.key(seed), 6)
    voltages = normal_values(key_of[0], (2, INPUTS, SAMPLES), 1.0, 6.0, ((1, 128),))
    filter_taps = normal_values(key_of[1], (TAPS, NCH), 0.25, 1.5, (), jnp.float32)
    station_flags = set_ends((jax.random.randint(key_of[2], (STATIONS,), 0, 8) < 7).astype(jnp.int32), jax.random.fold_in(key_of[2], 1), 0, 1)
    subband_lists = draw_subband_lists(jax.random.fold_in(key_of[5], 71), 0)
    subband_counts = draw_subband_counts(jax.random.fold_in(key_of[5], 71), 0)
    return {"voltages": voltages, "filter_taps": filter_taps, "station_flags": station_flags, "subband_lists": subband_lists, "subband_counts": subband_counts}


def cosine_tables(length):
    indices = jnp.arange(length, dtype=jnp.int32)
    products = indices[:, None] * indices[None, :] % length
    angles = products.astype(jnp.float32) * (2.0 * math.pi / length)
    return (jnp.cos(angles).astype(jnp.bfloat16), jnp.sin(angles).astype(jnp.bfloat16))

def twiddles():
    row_index = jnp.arange(FIRST, dtype=jnp.int32)
    col_index = jnp.arange(SECOND, dtype=jnp.int32)
    products = row_index[:, None] * col_index[None, :] % NCH
    angles = products.astype(jnp.float32) * (2.0 * math.pi / NCH)
    return (jnp.cos(angles), jnp.sin(angles))

def mixed(left, right, form):
    return jnp.einsum(form, left.astype(jnp.float32), right.astype(jnp.float32))

def channelize(signal, weight, filter_taps, channel_ids):
    cosine_first, sine_first = cosine_tables(FIRST)
    cosine_second, sine_second = cosine_tables(SECOND)
    twiddle_cos, twiddle_sin = twiddles()
    segments = signal.reshape(2, SPECTRA + TAPS - 1, NCH)
    frame = jnp.zeros((2, SPECTRA, NCH), jnp.float32)
    for offset in range(TAPS):
        frame = frame + filter_taps[offset] * segments[:, offset:offset + SPECTRA].astype(jnp.float32)
    frame = frame.astype(jnp.bfloat16).reshape(2, SPECTRA, FIRST, SECOND)
    form_one = 'tab,ak->tkb'
    first_real = mixed(frame[0], cosine_first, form_one) + mixed(frame[1], sine_first, form_one)
    first_imag = mixed(frame[1], cosine_first, form_one) - mixed(frame[0], sine_first, form_one)
    rotated_real = (first_real * twiddle_cos + first_imag * twiddle_sin).astype(jnp.bfloat16)
    rotated_imag = (first_imag * twiddle_cos - first_real * twiddle_sin).astype(jnp.bfloat16)
    form_two = 'tkb,bm->tkm'
    scale = weight / math.sqrt(NCH)
    spec_real = (mixed(rotated_real, cosine_second, form_two) + mixed(rotated_imag, sine_second, form_two)) * scale
    spec_imag = (mixed(rotated_imag, cosine_second, form_two) - mixed(rotated_real, sine_second, form_two)) * scale
    both = jnp.stack([spec_real, spec_imag]).astype(jnp.bfloat16)
    ordered = jnp.transpose(both, (0, 1, 3, 2)).reshape(2, SPECTRA, NCH)
    return jnp.take(ordered, channel_ids, axis=2)

def reference(voltages, filter_taps, station_flags, subband_lists, subband_counts):
    offsets = jnp.arange(SUBW, dtype=jnp.int32)
    channel_ids = (subband_lists[:, :, None] * SUBW + offsets[None, None, :]).reshape(-1).astype(jnp.int32)
    input_flags = jnp.repeat(station_flags, 2).astype(jnp.float32)

    def one_input(position):
        signal = lax.dynamic_index_in_dim(voltages, position, 1, keepdims=False)
        weight = lax.dynamic_index_in_dim(input_flags, position, 0, keepdims=False)
        return channelize(signal, weight, filter_taps, channel_ids)
    selected = lax.map(one_input, jnp.arange(INPUTS, dtype=jnp.int32))
    blocks = selected.reshape(N_STN, INB, 2, SPECTRA, CHSEL)
    blocks = jnp.transpose(blocks, (0, 4, 3, 2, 1)).reshape(N_STN, CHSEL, SPECTRA, 2 * INB).astype(jnp.float32)
    slot_index = jnp.arange(CHSEL, dtype=jnp.int32)
    live_slots = (slot_index % CAPCH // SUBW < subband_counts[slot_index // CAPCH]).astype(jnp.float32)
    results = []
    for distance in range(NDIST):
        partner = jnp.roll(blocks, -distance, axis=0)
        gram = jnp.einsum('sfta,sftb->sfab', blocks, partner)
        real_part = gram[..., :INB, :INB] + gram[..., INB:, INB:]
        imag_part = gram[..., INB:, :INB] - gram[..., :INB, INB:]
        joined = jnp.concatenate([real_part, imag_part], axis=-1)
        results.append(joined * live_slots[None, :, None, None] / SPECTRA)
    return jnp.stack(results, axis=1)
```

```python
import functools
import math

import jax
import jax.numpy as jnp
import numpy as np
from jax import lax
from jax.experimental import pallas as pl
from jax.experimental.pallas import tpu as pltpu
from jax.sharding import PartitionSpec as P

NCH = 8192
FIRST = 64
SECOND = 128
TAPS = 16
SPECTRA = 16
SUBW = 4
CAP = 16
SEGMENTS = SPECTRA + TAPS - 1
LOCAL = 8
LANES = SPECTRA * 2 * SUBW
CHUNK = 1024
VMEM = 48 * 1024 * 1024


def table(length, rows, cols):
    angles = (np.outer(np.arange(rows), np.arange(cols)) % length) * (2.0 * math.pi / length)
    return np.cos(angles), np.sin(angles)


def complex_block(cosine, sine):
    return np.block([[cosine, -sine], [sine, cosine]])


def channelize_kernel(*refs):
    volts = refs[:SEGMENTS]
    taps, first_w, twid, second_w, lists, scale, out, frames, picked, turned = refs[SEGMENTS:]
    step = pl.program_id(0)
    per_step = CHUNK // SECOND

    def filter_one(at, carry):
        lanes = pl.ds(pl.multiple_of(at * SECOND, SECOND), SECOND)
        row = step * per_step + at
        coeffs = [jnp.broadcast_to(taps[j : j + 1, lanes], (LOCAL, SECOND)) for j in range(TAPS)]
        for part in range(2):
            sums = {}
            for seg in range(SEGMENTS):
                value = volts[seg][part, :, lanes].astype(jnp.float32)
                for j in range(TAPS):
                    t = seg - j
                    if 0 <= t < SPECTRA:
                        term = coeffs[j] * value
                        sums[t] = sums[t] + term if t in sums else term
                if seg >= TAPS - 1:
                    t = seg - TAPS + 1
                    frames[part, t, pl.ds(row, LOCAL, stride=FIRST), :] = sums.pop(t)
        return carry

    lax.fori_loop(0, per_step, filter_one, 0)

    @pl.when(step == pl.num_programs(0) - 1)
    def transform():
        number_m = lists[0:1, :]
        number_k = lists[1:2, :]
        onehot = (lax.broadcasted_iota(jnp.int32, (SECOND, 128), 0) == number_m).astype(jnp.bfloat16)
        chosen = jnp.concatenate(
            [
                jnp.dot(second_w[:, q * SECOND : (q + 1) * SECOND], onehot, preferred_element_type=jnp.float32)
                for q in range(2)
            ],
            axis=1,
        ).astype(jnp.bfloat16)
        half = lax.broadcasted_iota(jnp.int32, (8, 128), 0) // SUBW
        masks = [number_k == 2 * v + half for v in range(FIRST // 8)]
        low = half == 0
        group = 4

        def one(index, carry):
            i = index // (SPECTRA // group)
            t0 = (index % (SPECTRA // group)) * group
            rows = pl.ds(pl.multiple_of(i * FIRST, FIRST), FIRST)
            block = jnp.concatenate(
                [
                    jnp.concatenate([frames[part, t0 + n, rows, :] for part in range(2)], axis=0)
                    for n in range(group)
                ],
                axis=1,
            ).astype(jnp.bfloat16)
            first = jnp.dot(first_w[...], block, preferred_element_type=jnp.float32)
            rotated = []
            for n in range(group):
                real = first[:FIRST, n * SECOND : (n + 1) * SECOND]
                imag = first[FIRST:, n * SECOND : (n + 1) * SECOND]
                cosine, sine = twid[0], twid[1]
                rotated.append(
                    jnp.concatenate([real * cosine + imag * sine, imag * cosine - real * sine], axis=1)
                )
            rotated = jnp.concatenate(rotated, axis=0).astype(jnp.bfloat16)
            second = jnp.dot(rotated, chosen, preferred_element_type=jnp.float32)
            for n in range(group):
                folded = []
                for q in range(2):
                    total = jnp.zeros((8, 128), jnp.float32)
                    for v in range(FIRST // 8):
                        piece = second[n * FIRST + v * 8 : n * FIRST + v * 8 + 8, q * 128 : q * 128 + 128]
                        total = jnp.where(masks[v], piece, total)
                    folded.append(total + pltpu.roll(total, SUBW, 0))
                picked[i, pl.ds(pl.multiple_of((t0 + n) * 8, 8), 8), :] = jnp.where(low, folded[0], folded[1])
            return carry

        lax.fori_loop(0, LOCAL * SPECTRA // group, one, 0)
        for i in range(LOCAL):
            turned[pl.ds(i, 128, stride=LOCAL), :] = picked[i].T * scale[i]
        values = turned[...].reshape(8, CAP, LOCAL, LANES).astype(jnp.bfloat16)
        out[0] = values
        out[1] = values


def channelize(voltages, filter_taps, station_flags, subband_lists):
    cos1, sin1 = table(FIRST, FIRST, FIRST)
    cos2, sin2 = table(SECOND, SECOND, SECOND)
    first_w = jnp.asarray(complex_block(cos1, sin1).T, jnp.bfloat16)
    second_w = jnp.asarray(complex_block(cos2, sin2), jnp.bfloat16)
    twid = jnp.asarray(np.stack(table(NCH, FIRST, SECOND)), jnp.float32)
    flat = subband_lists.reshape(-1)
    lists = jnp.stack([flat // (FIRST // SUBW), flat % (FIRST // SUBW)])
    scale = jnp.repeat(station_flags, 2).astype(jnp.float32) / math.sqrt(NCH)
    steps = NCH // CHUNK

    def whole(*shape):
        return pl.BlockSpec(shape, lambda n: (0,) * len(shape))

    def segment(seg):
        return pl.BlockSpec((2, LOCAL, CHUNK), lambda n: (0, 0, seg * steps + n))

    return pl.pallas_call(
        channelize_kernel,
        grid=(steps,),
        in_specs=[segment(seg) for seg in range(SEGMENTS)]
        + [
            pl.BlockSpec((TAPS, CHUNK), lambda n: (0, n)),
            whole(2 * FIRST, 2 * FIRST),
            whole(2, FIRST, SECOND),
            whole(2 * SECOND, 2 * SECOND),
            whole(2, 128),
            pl.BlockSpec(memory_space=pltpu.SMEM),
        ],
        out_specs=whole(2, 8, CAP, LOCAL, LANES),
        out_shape=jax.ShapeDtypeStruct((2, 8, CAP, LOCAL, LANES), jnp.bfloat16),
        scratch_shapes=[
            pltpu.VMEM((2, SPECTRA, LOCAL * FIRST, SECOND), jnp.float32),
            pltpu.VMEM((LOCAL, LANES, 128), jnp.float32),
            pltpu.VMEM((128 * LOCAL, LANES), jnp.float32),
        ],
        compiler_params=pltpu.CompilerParams(vmem_limit_bytes=VMEM),
        name="channelize",
    )(*([voltages] * SEGMENTS), filter_taps, first_w, twid, second_w, lists, scale)


BSLOTS = 4


def correlate_kernel(count, first_call, *refs):
    places, live, own = refs[:3]
    others = refs[3 : 3 + count]
    out, results, sems = refs[-3:]
    step = pl.program_id(0)
    steps = pl.num_programs(0)
    lane = lax.broadcasted_iota(jnp.int32, (64, LANES), 1)
    real_lane = lane // SUBW % 2 == 0
    buf = step % 2

    def copies(at, slot):
        rows = pl.ds(at * BSLOTS * SUBW, BSLOTS * SUBW)
        return [
            pltpu.make_async_copy(results.at[slot, n], out.at[places[n], rows], sems.at[slot, n])
            for n in range(count)
        ]

    @pl.when(step >= 2)
    def reuse():
        for copy in copies(step - 2, buf):
            copy.wait()

    for k in range(BSLOTS):
        factor = live[step * BSLOTS + k]
        mine = own[:, k].astype(jnp.float32).reshape(64, LANES) * factor
        crossed = jnp.where(real_lane, pltpu.roll(mine, LANES - SUBW, 1), -pltpu.roll(mine, SUBW, 1))
        left = jnp.concatenate(
            [
                jnp.concatenate(
                    [jnp.where(lane % SUBW == u, x, 0.0).astype(jnp.bfloat16) for x in (mine, crossed)], axis=1
                )
                for u in range(SUBW)
            ],
            axis=0,
        )
        zero = jnp.zeros((64, LANES), jnp.bfloat16)
        for at in range(0, count, 2):
            right = []
            for n in range(at, min(at + 2, count)):
                block = others[n][:, k].reshape(64, LANES)
                right += [jnp.concatenate([block, zero], axis=1), jnp.concatenate([zero, block], axis=1)]
            right = jnp.concatenate(right, axis=0)
            product = lax.dot_general(
                left, right, (((1,), (1,)), ((), ())), preferred_element_type=jnp.float32
            )
            for n in range(at, min(at + 2, count)):
                piece = product[:, (n - at) * 128 : (n - at + 1) * 128]
                results[buf, n, k * SUBW : (k + 1) * SUBW] = piece.reshape(SUBW, 64, 128)

    for copy in copies(step, buf):
        copy.start()

    @pl.when(step == steps - 1)
    def finish():
        for copy in copies(step - 1, 1 - buf) + copies(step, buf):
            copy.wait()


def correlate(total, places, live, own, others):
    count = len(others)
    block = pl.BlockSpec((8, BSLOTS, LOCAL, LANES), lambda n: (0, n, 0, 0))
    shape = jax.ShapeDtypeStruct((9, CAP * SUBW, 64, 128), jnp.float32)
    args = [places, live, own, *others]
    specs = [pl.BlockSpec(memory_space=pltpu.SMEM)] * 2 + [block] * (1 + count)
    aliases = {}
    if total is not None:
        aliases = {len(args): 0}
        args.append(total)
        specs.append(pl.BlockSpec(memory_space=pl.ANY))
    return pl.pallas_call(
        functools.partial(correlate_kernel, count, total is None),
        grid=(CAP // BSLOTS,),
        in_specs=specs,
        out_specs=pl.BlockSpec(memory_space=pl.ANY),
        out_shape=shape,
        scratch_shapes=[
            pltpu.VMEM((2, count, BSLOTS * SUBW, 64, 128), jnp.float32),
            pltpu.SemaphoreType.DMA((2, count)),
        ],
        input_output_aliases=aliases,
        compiler_params=pltpu.CompilerParams(vmem_limit_bytes=VMEM),
        name="correlate",
    )(*args)


def per_device(voltages, filter_taps, station_flags, subband_lists, subband_counts):
    stn = lax.axis_index("stn")
    row, col, core = stn // 8, stn // 2 % 4, stn % 2
    group = lax.axis_index("chan")
    count = lax.dynamic_index_in_dim(subband_counts, group, 0, keepdims=False)
    live = (jnp.arange(CAP, dtype=jnp.int32) < count).astype(jnp.float32) / SPECTRA

    selected = channelize(voltages, filter_taps, station_flags, subband_lists)
    selected = selected.reshape(16, CAP, LOCAL, LANES)
    members = [
        [(y * 8 + z * 2 + c) * 8 + g for y in range(2) for g in range(8)] for z in range(4) for c in range(2)
    ]
    rows = lax.all_to_all(selected, ("stn", "chan"), 0, 0, axis_index_groups=members, tiled=True)
    rows = rows.reshape(2, 8, CAP, LOCAL, LANES)

    def take(r):
        return lax.dynamic_index_in_dim(rows, r, 0, keepdims=False)

    def exchange(array, flip):
        return lax.ppermute(array, "stn", [(i, i ^ flip) for i in range(16)])

    own = take(row)
    far = take(1 - row)
    moved = {}
    for flip in (2, 1, 3):
        other = col ^ flip
        moved[flip] = exchange(jnp.where(col > other, own, far), flip * 2)
    spare = exchange(jnp.where(core == 0, far, own), 1)
    passed = {flip: exchange(moved[flip], 1) for flip in (1, 3, 2)}

    side = 1 - 2 * core
    ahead = {flip: 2 * ((col ^ flip) - col + 4) % 8 for flip in (1, 2, 3)}
    total = correlate(
        None, jnp.stack([0 * core, 8 + 0 * core, 1 + 6 * core]).astype(jnp.int32), live, own, [own, far, spare]
    )
    total = correlate(
        total,
        jnp.stack([ahead[1], ahead[3], ahead[1] + side, ahead[3] + side]).astype(jnp.int32),
        live,
        own,
        [moved[1], moved[3], passed[1], passed[3]],
    )
    total = correlate(
        total, jnp.stack([ahead[2], ahead[2] + side]).astype(jnp.int32), live, own, [moved[2], passed[2]]
    )
    return total[None]


def solution(mesh):
    placed = (P(None, ("stn", "chan"), None), P(), P(("stn", "chan")), P(), P())
    return jax.shard_map(
        per_device,
        mesh=mesh,
        in_specs=placed,
        out_specs=P("stn", None, "chan", None, None),
        check_vma=False,
    )
```

```python
import functools
import math

import jax
import jax.numpy as jnp
import numpy as np
from jax import lax
from jax.experimental import pallas as pl
from jax.experimental.pallas import tpu as pltpu
from jax.sharding import PartitionSpec as P

NCH = 8192
FIRST = 64
SECOND = 128
TAPS = 16
SPECTRA = 16
SUBW = 4
CAP = 16
SEGMENTS = SPECTRA + TAPS - 1
LOCAL = 8
LANES = SPECTRA * 2 * SUBW
CHUNK = 1024
PITCH = FIRST + 8
GROUP = 8
UNROLL = 8
VMEM = 48 * 1024 * 1024
VMEM_ALL = 60 * 1024 * 1024


def table(length, rows, cols):
    angles = (np.outer(np.arange(rows), np.arange(cols)) % length) * (2.0 * math.pi / length)
    return np.cos(angles), np.sin(angles)


def complex_block(cosine, sine):
    return np.block([[cosine, -sine], [sine, cosine]])


def channelize_kernel(*refs):
    volts, taps, first_hbm, twid_hbm, second_hbm, lists, flags, out = refs[:8]
    frames, picked, turned, first_w, twid, second_w, sems = refs[8:]
    step = pl.program_id(0)
    per_step = CHUNK // SECOND

    copies = [
        pltpu.make_async_copy(source, target, sems.at[n])
        for n, (source, target) in enumerate(
            ((first_hbm, first_w), (twid_hbm, twid), (second_hbm, second_w))
        )
    ]

    @pl.when(step == 0)
    def fetch():
        for copy in copies:
            copy.start()

    def filter_one(at, carry):
        lanes = pl.ds(pl.multiple_of(at * SECOND, SECOND), SECOND)
        row = step * per_step + at
        coeffs = [jnp.broadcast_to(taps[j : j + 1, lanes], (LOCAL, SECOND)) for j in range(TAPS)]
        for part in range(2):
            sums = {}
            for seg in range(SEGMENTS):
                value = volts[part, seg, :, lanes].astype(jnp.float32)
                for j in range(TAPS):
                    t = seg - j
                    if 0 <= t < SPECTRA:
                        term = coeffs[j] * value
                        sums[t] = sums[t] + term if t in sums else term
                if seg >= TAPS - 1:
                    t = seg - TAPS + 1
                    frames[part, t, pl.ds(row, LOCAL, stride=PITCH), :] = sums.pop(t)
        return carry

    lax.fori_loop(0, per_step, filter_one, 0, unroll=2)

    @pl.when(step == pl.num_programs(0) - 1)
    def transform():
        for copy in copies:
            copy.wait()
        spread = lax.broadcasted_iota(jnp.int32, (CAP, 128), 1) % CAP == lax.broadcasted_iota(
            jnp.int32, (CAP, 128), 0
        )
        spread = spread.astype(jnp.bfloat16)
        diagonal = lax.broadcasted_iota(jnp.int32, (8, 128), 1) // CAP == lax.broadcasted_iota(
            jnp.int32, (8, 128), 0
        )

        def along_lanes(numbers):
            full = jnp.dot(numbers.astype(jnp.bfloat16), spread, preferred_element_type=jnp.float32)
            return jnp.sum(jnp.where(diagonal, full, 0.0), axis=0, keepdims=True).astype(jnp.int32)

        number_m = along_lanes(lists[...] // (FIRST // SUBW))
        number_k = along_lanes(lists[...] % (FIRST // SUBW))
        onehot = (lax.broadcasted_iota(jnp.int32, (SECOND, 128), 0) == number_m).astype(jnp.bfloat16)
        chosen = jnp.concatenate(
            [
                jnp.dot(second_w[:, q * SECOND : (q + 1) * SECOND], onehot, preferred_element_type=jnp.float32)
                for q in range(2)
            ],
            axis=1,
        ).astype(jnp.bfloat16)
        half = lax.broadcasted_iota(jnp.int32, (8, 128), 0) // SUBW
        masks = [number_k == 2 * v + half for v in range(FIRST // 8)]
        low = half == 0
        group = GROUP

        def one(index, carry):
            i = index // (SPECTRA // group)
            t0 = (index % (SPECTRA // group)) * group
            rows = pl.ds(pl.multiple_of(i * PITCH, 8), FIRST)
            block = jnp.concatenate(
                [
                    jnp.concatenate([frames[part, t0 + n, rows, :] for part in range(2)], axis=0)
                    for n in range(group)
                ],
                axis=1,
            ).astype(jnp.bfloat16)
            first = jnp.dot(first_w[...], block, preferred_element_type=jnp.float32)
            rotated = []
            for n in range(group):
                real = first[:FIRST, n * SECOND : (n + 1) * SECOND]
                imag = first[FIRST:, n * SECOND : (n + 1) * SECOND]
                cosine, sine = twid[0], twid[1]
                rotated.append(
                    jnp.concatenate([real * cosine + imag * sine, imag * cosine - real * sine], axis=1)
                )
            rotated = jnp.concatenate(rotated, axis=0).astype(jnp.bfloat16)
            second = jnp.dot(rotated, chosen, preferred_element_type=jnp.float32)
            for n in range(group):
                folded = []
                for q in range(2):
                    total = jnp.zeros((8, 128), jnp.float32)
                    for v in range(FIRST // 8):
                        piece = second[n * FIRST + v * 8 : n * FIRST + v * 8 + 8, q * 128 : q * 128 + 128]
                        total = jnp.where(masks[v], piece, total)
                    folded.append(total + pltpu.roll(total, SUBW, 0))
                picked[i, pl.ds(pl.multiple_of((t0 + n) * 8, 8), 8), :] = jnp.where(low, folded[0], folded[1])
            return carry

        lax.fori_loop(0, LOCAL * SPECTRA // group, one, 0, unroll=UNROLL)
        for i in range(LOCAL):
            turned[pl.ds(i, 128, stride=LOCAL), :] = picked[i].T * (flags[i // 2].astype(jnp.float32) * (1.0 / math.sqrt(NCH)))
        values = turned[...].reshape(8, CAP, LOCAL, LANES).astype(jnp.bfloat16)
        out[0] = values
        out[1] = values


def channelize(voltages, filter_taps, station_flags, subband_lists):
    cos1, sin1 = table(FIRST, FIRST, FIRST)
    cos2, sin2 = table(SECOND, SECOND, SECOND)
    first_w = jnp.asarray(complex_block(cos1, sin1).T, jnp.bfloat16)
    second_w = jnp.asarray(complex_block(cos2, sin2), jnp.bfloat16)
    twid = jnp.asarray(np.stack(table(NCH, FIRST, SECOND)), jnp.float32)
    steps = NCH // CHUNK
    volts = voltages.reshape(2, LOCAL, SEGMENTS, NCH).transpose(0, 2, 1, 3)

    def whole(*shape):
        return pl.BlockSpec(shape, lambda n: (0,) * len(shape))

    hbm = pl.BlockSpec(memory_space=pltpu.HBM)
    return pl.pallas_call(
        channelize_kernel,
        grid=(steps,),
        in_specs=[
            pl.BlockSpec((2, SEGMENTS, LOCAL, CHUNK), lambda n: (0, 0, 0, n)),
            pl.BlockSpec((TAPS, CHUNK), lambda n: (0, n)),
            hbm,
            hbm,
            hbm,
            whole(8, CAP),
            pl.BlockSpec(memory_space=pltpu.SMEM),
        ],
        out_specs=whole(2, 8, CAP, LOCAL, LANES),
        out_shape=jax.ShapeDtypeStruct((2, 8, CAP, LOCAL, LANES), jnp.bfloat16),
        scratch_shapes=[
            pltpu.VMEM((2, SPECTRA, LOCAL * PITCH, SECOND), jnp.float32),
            pltpu.VMEM((LOCAL, LANES, 128), jnp.float32),
            pltpu.VMEM((128 * LOCAL, LANES), jnp.float32),
            pltpu.VMEM((2 * FIRST, 2 * FIRST), jnp.bfloat16),
            pltpu.VMEM((2, FIRST, SECOND), jnp.float32),
            pltpu.VMEM((2 * SECOND, 2 * SECOND), jnp.bfloat16),
            pltpu.SemaphoreType.DMA((3,)),
        ],
        compiler_params=pltpu.CompilerParams(vmem_limit_bytes=VMEM_ALL),
        name="channelize",
    )(volts, filter_taps, first_w, twid, second_w, subband_lists, station_flags)


BSLOTS = 8


def correlate_kernel(count, *refs):
    places, counts, own = refs[:3]
    others = refs[3 : 3 + count]
    out, results, sems = refs[-3:]
    step = pl.program_id(0)
    steps = pl.num_programs(0)
    lane = lax.broadcasted_iota(jnp.int32, (64, LANES), 1)
    real_lane = lane // SUBW % 2 == 0
    buf = step % 2

    def copies(at, slot):
        rows = pl.ds(at * BSLOTS * SUBW, BSLOTS * SUBW)
        return [
            pltpu.make_async_copy(results.at[slot, n], out.at[places[n + 1], rows], sems.at[slot, n])
            for n in range(count)
        ]

    @pl.when(step >= 2)
    def reuse():
        for copy in copies(step - 2, buf):
            copy.wait()

    for k in range(BSLOTS):
        factor = jnp.where(step * BSLOTS + k < counts[places[0]], 1.0 / SPECTRA, 0.0)
        mine = own[:, k].astype(jnp.float32).reshape(64, LANES) * factor
        crossed = jnp.where(real_lane, pltpu.roll(mine, LANES - SUBW, 1), -pltpu.roll(mine, SUBW, 1))
        left = jnp.concatenate(
            [
                jnp.concatenate(
                    [jnp.where(lane % SUBW == u, x, 0.0).astype(jnp.bfloat16) for x in (mine, crossed)], axis=1
                )
                for u in range(SUBW)
            ],
            axis=0,
        )
        zero = jnp.zeros((64, LANES), jnp.bfloat16)
        for at in range(0, count, 2):
            right = []
            for n in range(at, min(at + 2, count)):
                block = others[n][:, k].reshape(64, LANES)
                right += [jnp.concatenate([block, zero], axis=1), jnp.concatenate([zero, block], axis=1)]
            right = jnp.concatenate(right, axis=0)
            product = lax.dot_general(
                left, right, (((1,), (1,)), ((), ())), preferred_element_type=jnp.float32
            )
            for n in range(at, min(at + 2, count)):
                piece = product[:, (n - at) * 128 : (n - at + 1) * 128]
                results[buf, n, k * SUBW : (k + 1) * SUBW] = piece.reshape(SUBW, 64, 128)

    for copy in copies(step, buf):
        copy.start()

    @pl.when(step == steps - 1)
    def finish():
        for copy in copies(step - 1, 1 - buf) + copies(step, buf):
            copy.wait()


def correlate(total, group, counts, own, pairs):
    places = jnp.stack([group] + [distance for distance, _ in pairs]).astype(jnp.int32)
    others = [block for _, block in pairs]
    count = len(others)
    block = pl.BlockSpec((8, BSLOTS, LOCAL, LANES), lambda n: (0, n, 0, 0))
    shape = jax.ShapeDtypeStruct((9, CAP * SUBW, 64, 128), jnp.float32)
    args = [places, counts, own, *others]
    specs = [pl.BlockSpec(memory_space=pltpu.SMEM)] * 2 + [block] * (1 + count)
    aliases = {}
    if total is not None:
        aliases = {len(args): 0}
        args.append(total)
        specs.append(pl.BlockSpec(memory_space=pl.ANY))
    return pl.pallas_call(
        functools.partial(correlate_kernel, count),
        grid=(CAP // BSLOTS,),
        in_specs=specs,
        out_specs=pl.BlockSpec(memory_space=pl.ANY),
        out_shape=shape,
        scratch_shapes=[
            pltpu.VMEM((2, count, BSLOTS * SUBW, 64, 128), jnp.float32),
            pltpu.SemaphoreType.DMA((2, count)),
        ],
        input_output_aliases=aliases,
        compiler_params=pltpu.CompilerParams(vmem_limit_bytes=VMEM),
        name="correlate",
    )(*args)


def per_device(voltages, filter_taps, station_flags, subband_lists, subband_counts):
    stn = lax.axis_index("stn")
    row, col, core = stn // 8, stn // 2 % 4, stn % 2
    group = lax.axis_index("chan")

    selected = channelize(voltages, filter_taps, station_flags, subband_lists)
    selected = selected.reshape(16, CAP, LOCAL, LANES)
    members = [
        [(y * 8 + z * 2 + c) * 8 + g for y in range(2) for g in range(8)] for z in range(4) for c in range(2)
    ]
    rows = lax.all_to_all(selected, ("stn", "chan"), 0, 0, axis_index_groups=members, tiled=True)
    rows = rows.reshape(2, 8, CAP, LOCAL, LANES)

    def take(r):
        return lax.dynamic_index_in_dim(rows, r, 0, keepdims=False)

    def exchange(array, flip):
        return lax.ppermute(array, "stn", [(i, i ^ flip) for i in range(16)])

    own = take(row)
    far = take(1 - row)
    moved = {}
    for flip in (2, 1, 3):
        other = col ^ flip
        moved[flip] = exchange(jnp.where(col > other, own, far), flip * 2)
    spare = exchange(jnp.where(core == 0, far, own), 1)

    side = 1 - 2 * core
    ahead = {flip: 2 * ((col ^ flip) - col + 4) % 8 for flip in (1, 2, 3)}
    join = functools.partial(correlate, group=group, counts=subband_counts, own=own)
    total = join(None, pairs=[(0 * core, own), (0 * core + 8, far), (1 + 6 * core, spare)])
    for flips in ((1, 3), (2,)):
        arrived = [moved[flip] for flip in flips]
        *arrived, total = lax.optimization_barrier((*arrived, total))
        pairs = []
        for flip, block in zip(flips, arrived):
            pairs += [(ahead[flip], block), (ahead[flip] + side, exchange(block, 1))]
        total = join(total, pairs=pairs)
    return total[None]


def solution(mesh):
    placed = (P(None, ("stn", "chan"), None), P(), P(("stn", "chan")), P(), P())
    return jax.shard_map(
        per_device,
        mesh=mesh,
        in_specs=placed,
        out_specs=P("stn", None, "chan", None, None),
        check_vma=False,
    )
```

```python
import functools
import math

import jax
import jax.numpy as jnp
import numpy as np
from jax import lax
from jax.experimental import pallas as pl
from jax.experimental.pallas import tpu as pltpu
from jax.sharding import PartitionSpec as P

NCH = 8192
FIRST = 64
SECOND = 128
TAPS = 16
SPECTRA = 16
SUBW = 4
CAP = 16
SEGMENTS = SPECTRA + TAPS - 1
LOCAL = 8
LANES = SPECTRA * 2 * SUBW
CHUNK = 1024
PITCH = FIRST + 8
GROUP = 8
UNROLL = 8
VMEM = 48 * 1024 * 1024
VMEM_ALL = 60 * 1024 * 1024


def table(length, rows, cols):
    angles = (np.outer(np.arange(rows), np.arange(cols)) % length) * (2.0 * math.pi / length)
    return np.cos(angles), np.sin(angles)


def complex_block(cosine, sine):
    return np.block([[cosine, -sine], [sine, cosine]])


def channelize_kernel(*refs):
    volts, taps, first_hbm, twid_hbm, second_hbm, lists, flags, out = refs[:8]
    frames, picked, turned, first_w, twid, second_w, sems = refs[8:]
    step = pl.program_id(0)
    per_step = CHUNK // SECOND

    copies = [
        pltpu.make_async_copy(source, target, sems.at[n])
        for n, (source, target) in enumerate(
            ((first_hbm, first_w), (twid_hbm, twid), (second_hbm, second_w))
        )
    ]

    @pl.when(step == 0)
    def fetch():
        for copy in copies:
            copy.start()

    def filter_one(at, carry):
        lanes = pl.ds(pl.multiple_of(at * SECOND, SECOND), SECOND)
        row = step * per_step + at
        coeffs = [jnp.broadcast_to(taps[j : j + 1, lanes], (LOCAL, SECOND)) for j in range(TAPS)]
        for part in range(2):
            sums = {}
            for seg in range(SEGMENTS):
                value = volts[part, seg, :, lanes].astype(jnp.float32)
                for j in range(TAPS):
                    t = seg - j
                    if 0 <= t < SPECTRA:
                        term = coeffs[j] * value
                        sums[t] = sums[t] + term if t in sums else term
                if seg >= TAPS - 1:
                    t = seg - TAPS + 1
                    frames[part, t, pl.ds(row, LOCAL, stride=PITCH), :] = sums.pop(t)
        return carry

    lax.fori_loop(0, per_step, filter_one, 0, unroll=2)

    @pl.when(step == pl.num_programs(0) - 1)
    def transform():
        for copy in copies:
            copy.wait()
        spread = lax.broadcasted_iota(jnp.int32, (CAP, 128), 1) % CAP == lax.broadcasted_iota(
            jnp.int32, (CAP, 128), 0
        )
        spread = spread.astype(jnp.bfloat16)
        diagonal = lax.broadcasted_iota(jnp.int32, (8, 128), 1) // CAP == lax.broadcasted_iota(
            jnp.int32, (8, 128), 0
        )

        def along_lanes(numbers):
            full = jnp.dot(numbers.astype(jnp.bfloat16), spread, preferred_element_type=jnp.float32)
            return jnp.sum(jnp.where(diagonal, full, 0.0), axis=0, keepdims=True).astype(jnp.int32)

        number_m = along_lanes(lists[...] // (FIRST // SUBW))
        number_k = along_lanes(lists[...] % (FIRST // SUBW))
        onehot = (lax.broadcasted_iota(jnp.int32, (SECOND, 128), 0) == number_m).astype(jnp.bfloat16)
        chosen = jnp.concatenate(
            [
                jnp.dot(second_w[:, q * SECOND : (q + 1) * SECOND], onehot, preferred_element_type=jnp.float32)
                for q in range(2)
            ],
            axis=1,
        ).astype(jnp.bfloat16)
        half = lax.broadcasted_iota(jnp.int32, (8, 128), 0) // SUBW
        masks = [number_k == 2 * v + half for v in range(FIRST // 8)]
        low = half == 0
        group = GROUP

        def one(index, carry):
            i = index // (SPECTRA // group)
            t0 = (index % (SPECTRA // group)) * group
            rows = pl.ds(pl.multiple_of(i * PITCH, 8), FIRST)
            block = jnp.concatenate(
                [
                    jnp.concatenate([frames[part, t0 + n, rows, :] for part in range(2)], axis=0)
                    for n in range(group)
                ],
                axis=1,
            ).astype(jnp.bfloat16)
            first = jnp.dot(first_w[...], block, preferred_element_type=jnp.float32)
            rotated = []
            for n in range(group):
                real = first[:FIRST, n * SECOND : (n + 1) * SECOND]
                imag = first[FIRST:, n * SECOND : (n + 1) * SECOND]
                cosine, sine = twid[0], twid[1]
                rotated.append(
                    jnp.concatenate([real * cosine + imag * sine, imag * cosine - real * sine], axis=1)
                )
            rotated = jnp.concatenate(rotated, axis=0).astype(jnp.bfloat16)
            second = jnp.dot(rotated, chosen, preferred_element_type=jnp.float32)
            for n in range(group):
                folded = []
                for q in range(2):
                    total = jnp.zeros((8, 128), jnp.float32)
                    for v in range(FIRST // 8):
                        piece = second[n * FIRST + v * 8 : n * FIRST + v * 8 + 8, q * 128 : q * 128 + 128]
                        total = jnp.where(masks[v], piece, total)
                    folded.append(total + pltpu.roll(total, SUBW, 0))
                picked[i, pl.ds(pl.multiple_of((t0 + n) * 8, 8), 8), :] = jnp.where(low, folded[0], folded[1])
            return carry

        lax.fori_loop(0, LOCAL * SPECTRA // group, one, 0, unroll=UNROLL)
        for i in range(LOCAL):
            turned[pl.ds(i, 128, stride=LOCAL), :] = picked[i].T * (flags[i // 2].astype(jnp.float32) * (1.0 / math.sqrt(NCH)))
        values = turned[...].reshape(8, CAP, LOCAL, LANES).astype(jnp.bfloat16)
        out[0] = values
        out[1] = values


def channelize(voltages, filter_taps, station_flags, subband_lists):
    cos1, sin1 = table(FIRST, FIRST, FIRST)
    cos2, sin2 = table(SECOND, SECOND, SECOND)
    first_w = jnp.asarray(complex_block(cos1, sin1).T, jnp.bfloat16)
    second_w = jnp.asarray(complex_block(cos2, sin2), jnp.bfloat16)
    twid = jnp.asarray(np.stack(table(NCH, FIRST, SECOND)), jnp.float32)
    steps = NCH // CHUNK
    volts = voltages.reshape(2, LOCAL, SEGMENTS, NCH).transpose(0, 2, 1, 3)

    def whole(*shape):
        return pl.BlockSpec(shape, lambda n: (0,) * len(shape))

    hbm = pl.BlockSpec(memory_space=pltpu.HBM)
    return pl.pallas_call(
        channelize_kernel,
        grid=(steps,),
        in_specs=[
            pl.BlockSpec((2, SEGMENTS, LOCAL, CHUNK), lambda n: (0, 0, 0, n)),
            pl.BlockSpec((TAPS, CHUNK), lambda n: (0, n)),
            hbm,
            hbm,
            hbm,
            whole(8, CAP),
            pl.BlockSpec(memory_space=pltpu.SMEM),
        ],
        out_specs=whole(2, 8, CAP, LOCAL, LANES),
        out_shape=jax.ShapeDtypeStruct((2, 8, CAP, LOCAL, LANES), jnp.bfloat16),
        scratch_shapes=[
            pltpu.VMEM((2, SPECTRA, LOCAL * PITCH, SECOND), jnp.float32),
            pltpu.VMEM((LOCAL, LANES, 128), jnp.float32),
            pltpu.VMEM((128 * LOCAL, LANES), jnp.float32),
            pltpu.VMEM((2 * FIRST, 2 * FIRST), jnp.bfloat16),
            pltpu.VMEM((2, FIRST, SECOND), jnp.float32),
            pltpu.VMEM((2 * SECOND, 2 * SECOND), jnp.bfloat16),
            pltpu.SemaphoreType.DMA((3,)),
        ],
        compiler_params=pltpu.CompilerParams(vmem_limit_bytes=VMEM_ALL),
        name="channelize",
    )(volts, filter_taps, first_w, twid, second_w, subband_lists, station_flags)


def correlate_kernel(count, *refs):
    places, counts, own = refs[:3]
    others = refs[3 : 3 + count]
    out, results, sems = refs[-3:]
    lane = lax.broadcasted_iota(jnp.int32, (64, LANES), 1)
    real_lane = lane // SUBW % 2 == 0
    zero = jnp.zeros((64, LANES), jnp.bfloat16)

    def one_slot(slot, carry):
        factor = jnp.where(slot < counts[places[0]], 1.0 / SPECTRA, 0.0)
        mine = own[:, slot].astype(jnp.float32).reshape(64, LANES) * factor
        crossed = jnp.where(real_lane, pltpu.roll(mine, LANES - SUBW, 1), -pltpu.roll(mine, SUBW, 1))
        left = jnp.concatenate(
            [
                jnp.concatenate(
                    [jnp.where(lane % SUBW == u, x, 0.0).astype(jnp.bfloat16) for x in (mine, crossed)], axis=1
                )
                for u in range(SUBW)
            ],
            axis=0,
        )
        rows = pl.ds(slot * SUBW, SUBW)
        for at in range(0, count, 2):
            right = []
            for n in range(at, min(at + 2, count)):
                block = others[n][:, slot].reshape(64, LANES)
                right += [jnp.concatenate([block, zero], axis=1), jnp.concatenate([zero, block], axis=1)]
            right = jnp.concatenate(right, axis=0)
            product = lax.dot_general(
                left, right, (((1,), (1,)), ((), ())), preferred_element_type=jnp.float32
            )
            for n in range(at, min(at + 2, count)):
                piece = product[:, (n - at) * 128 : (n - at + 1) * 128]
                results[n, rows] = piece.reshape(SUBW, 64, 128)
        for n in range(count):
            pltpu.make_async_copy(results.at[n, rows], out.at[places[n + 1], rows], sems.at[n]).start()
        return carry

    lax.fori_loop(0, CAP, one_slot, 0, unroll=CUNROLL)
    for n in range(count):
        pltpu.make_async_copy(results.at[n], out.at[places[n + 1]], sems.at[n]).wait()


CUNROLL = 4


def correlate(total, group, counts, own, pairs):
    places = jnp.stack([group] + [distance for distance, _ in pairs]).astype(jnp.int32)
    others = [block for _, block in pairs]
    count = len(others)
    args = [places, counts, own, *others]
    specs = [pl.BlockSpec(memory_space=pltpu.SMEM)] * 2 + [pl.BlockSpec(memory_space=pltpu.VMEM)] * (1 + count)
    aliases = {}
    if total is not None:
        aliases = {len(args): 0}
        args.append(total)
        specs.append(pl.BlockSpec(memory_space=pl.ANY))
    return pl.pallas_call(
        functools.partial(correlate_kernel, count),
        in_specs=specs,
        out_specs=pl.BlockSpec(memory_space=pl.ANY),
        out_shape=jax.ShapeDtypeStruct((9, CAP * SUBW, 64, 128), jnp.float32),
        scratch_shapes=[
            pltpu.VMEM((count, CAP * SUBW, 64, 128), jnp.float32),
            pltpu.SemaphoreType.DMA((count,)),
        ],
        input_output_aliases=aliases,
        compiler_params=pltpu.CompilerParams(vmem_limit_bytes=VMEM),
        name="correlate",
    )(*args)


def per_device(voltages, filter_taps, station_flags, subband_lists, subband_counts):
    stn = lax.axis_index("stn")
    row, col, core = stn // 8, stn // 2 % 4, stn % 2
    group = lax.axis_index("chan")

    selected = channelize(voltages, filter_taps, station_flags, subband_lists)
    selected = selected.reshape(16, CAP, LOCAL, LANES)
    members = [
        [(y * 8 + z * 2 + c) * 8 + g for y in range(2) for g in range(8)] for z in range(4) for c in range(2)
    ]
    rows = lax.all_to_all(selected, ("stn", "chan"), 0, 0, axis_index_groups=members, tiled=True)
    rows = rows.reshape(2, 8, CAP, LOCAL, LANES)

    def take(r):
        return lax.dynamic_index_in_dim(rows, r, 0, keepdims=False)

    def exchange(array, flip):
        return lax.ppermute(array, "stn", [(i, i ^ flip) for i in range(16)])

    own = take(row)
    far = take(1 - row)
    moved = {}
    for flip in (2, 1, 3):
        other = col ^ flip
        moved[flip] = exchange(jnp.where(col > other, own, far), flip * 2)
    spare = exchange(jnp.where(core == 0, far, own), 1)

    side = 1 - 2 * core
    ahead = {flip: 2 * ((col ^ flip) - col + 4) % 8 for flip in (1, 2, 3)}
    join = functools.partial(correlate, group=group, counts=subband_counts, own=own)
    total = join(None, pairs=[(0 * core, own), (0 * core + 8, far), (1 + 6 * core, spare)])
    *arrived, total = lax.optimization_barrier((*(moved[flip] for flip in (1, 3, 2)), total))
    pairs = []
    for flip, block in zip((1, 3, 2), arrived):
        pairs += [(ahead[flip], block), (ahead[flip] + side, exchange(block, 1))]
    total = join(total, pairs=pairs)
    return total[None]


def solution(mesh):
    placed = (P(None, ("stn", "chan"), None), P(), P(("stn", "chan")), P(), P())
    return jax.shard_map(
        per_device,
        mesh=mesh,
        in_specs=placed,
        out_specs=P("stn", None, "chan", None, None),
        check_vma=False,
    )
```

```python
import functools
import math

import jax
import jax.numpy as jnp
import numpy as np
from jax import lax
from jax.experimental import pallas as pl
from jax.experimental.pallas import tpu as pltpu
from jax.sharding import PartitionSpec as P

NCH = 8192
FIRST = 64
SECOND = 128
TAPS = 16
SPECTRA = 16
SUBW = 4
CAP = 16
SEGMENTS = SPECTRA + TAPS - 1
LOCAL = 8
LANES = SPECTRA * 2 * SUBW
CHUNKS = (256, 256, 512, 1024, 2048, 2048, 2048)
FUNROLL = 2
DIRECT = 4
PITCH = FIRST + 8
GROUP = 8
UNROLL = 8
VMEM = 48 * 1024 * 1024
VMEM_ALL = 60 * 1024 * 1024


def table(length, rows, cols):
    angles = (np.outer(np.arange(rows), np.arange(cols)) % length) * (2.0 * math.pi / length)
    return np.cos(angles), np.sin(angles)


def complex_block(cosine, sine):
    return np.block([[cosine, -sine], [sine, cosine]])


def split_taps(taps):
    half = len(taps) // 2
    if len(taps) <= DIRECT:
        return taps
    low, high = taps[:half], taps[half:]
    return split_taps(low), split_taps(high), split_taps([a + b for a, b in zip(low, high)])


def sliding(tree, values, start=None):
    length = (len(values) + 1) // 2
    if isinstance(tree, list):
        totals = []
        for t in range(length):
            total = None if start is None else start[t]
            for j in range(length):
                term = tree[j] * values[t + j]
                total = term if total is None else total + term
            totals.append(total)
        return totals
    low, high, both = tree
    half = length // 2
    span = range(length - 1)
    shared = sliding(both, values[half : half + length - 1])
    first = shared if start is None else [a + b for a, b in zip(start[:half], shared)]
    second = shared if start is None else [a + b for a, b in zip(start[half:], shared)]
    return sliding(low, [values[n] - values[n + half] for n in span], first) + sliding(
        high, [values[n + length] - values[n + half] for n in span], second
    )


def channelize_kernel(*refs):
    volts_hbm, taps_hbm, first_hbm, twid_hbm, second_hbm, lists, flags, out = refs[:8]
    frames, picked, turned, first_w, twid, second_w, volts, taps, sems, fetched = refs[8:]

    copies = [
        pltpu.make_async_copy(source, target, sems.at[n])
        for n, (source, target) in enumerate(
            ((first_hbm, first_w), (twid_hbm, twid), (second_hbm, second_w))
        )
    ]

    starts = [sum(CHUNKS[:n]) for n in range(len(CHUNKS))]

    def pieces(n):
        lanes = pl.ds(starts[n], CHUNKS[n])
        return (
            pltpu.make_async_copy(taps_hbm.at[:, lanes], taps.at[:, lanes], fetched.at[n, 0]),
            pltpu.make_async_copy(
                volts_hbm.at[:, :, :, lanes], volts.at[:, :, :, lanes], fetched.at[n, 1]
            ),
        )

    for n in range(len(CHUNKS)):
        for copy in pieces(n):
            copy.start()
    for copy in copies:
        copy.start()

    def filter_one(at, carry):
        lanes = pl.ds(pl.multiple_of(at * SECOND, SECOND), SECOND)
        row = at
        coeffs = [jnp.broadcast_to(taps[j : j + 1, lanes], (LOCAL, SECOND)) for j in range(TAPS)]
        tree = split_taps(coeffs)
        for part in range(2):
            values = [volts[part, seg, :, lanes].astype(jnp.float32) for seg in range(SEGMENTS)]
            for t, total in enumerate(sliding(tree, values)):
                frames[part, t, pl.ds(row, LOCAL, stride=PITCH), :] = total
        return carry

    for n in range(len(CHUNKS)):
        for copy in pieces(n):
            copy.wait()
        first_row = starts[n] // SECOND
        lax.fori_loop(first_row, first_row + CHUNKS[n] // SECOND, filter_one, 0, unroll=FUNROLL)

    for copy in copies:
        copy.wait()
    spread = lax.broadcasted_iota(jnp.int32, (CAP, 128), 1) % CAP == lax.broadcasted_iota(
        jnp.int32, (CAP, 128), 0
    )
    spread = spread.astype(jnp.bfloat16)
    diagonal = lax.broadcasted_iota(jnp.int32, (8, 128), 1) // CAP == lax.broadcasted_iota(
        jnp.int32, (8, 128), 0
    )

    def along_lanes(numbers):
        full = jnp.dot(numbers.astype(jnp.bfloat16), spread, preferred_element_type=jnp.float32)
        return jnp.sum(jnp.where(diagonal, full, 0.0), axis=0, keepdims=True).astype(jnp.int32)

    number_m = along_lanes(lists[...] // (FIRST // SUBW))
    number_k = along_lanes(lists[...] % (FIRST // SUBW))
    onehot = (lax.broadcasted_iota(jnp.int32, (SECOND, 128), 0) == number_m).astype(jnp.bfloat16)
    chosen = jnp.concatenate(
        [
            jnp.dot(second_w[:, q * SECOND : (q + 1) * SECOND], onehot, preferred_element_type=jnp.float32)
            for q in range(2)
        ],
        axis=1,
    ).astype(jnp.bfloat16)
    half = lax.broadcasted_iota(jnp.int32, (8, 128), 0) // SUBW
    masks = [number_k == 2 * v + half for v in range(FIRST // 8)]
    low = half == 0
    group = GROUP

    def one(index, carry):
        i = index // (SPECTRA // group)
        t0 = (index % (SPECTRA // group)) * group
        rows = pl.ds(pl.multiple_of(i * PITCH, 8), FIRST)
        block = jnp.concatenate(
            [
                jnp.concatenate([frames[part, t0 + n, rows, :] for part in range(2)], axis=0)
                for n in range(group)
            ],
            axis=1,
        ).astype(jnp.bfloat16)
        first = jnp.dot(first_w[...], block, preferred_element_type=jnp.float32)
        rotated = []
        for n in range(group):
            real = first[:FIRST, n * SECOND : (n + 1) * SECOND]
            imag = first[FIRST:, n * SECOND : (n + 1) * SECOND]
            cosine, sine = twid[0], twid[1]
            rotated.append(
                jnp.concatenate([real * cosine + imag * sine, imag * cosine - real * sine], axis=1)
            )
        rotated = jnp.concatenate(rotated, axis=0).astype(jnp.bfloat16)
        second = jnp.dot(rotated, chosen, preferred_element_type=jnp.float32)
        for n in range(group):
            folded = []
            for q in range(2):
                total = jnp.zeros((8, 128), jnp.float32)
                for v in range(FIRST // 8):
                    piece = second[n * FIRST + v * 8 : n * FIRST + v * 8 + 8, q * 128 : q * 128 + 128]
                    total = jnp.where(masks[v], piece, total)
                folded.append(total + pltpu.roll(total, SUBW, 0))
            picked[i, pl.ds(pl.multiple_of((t0 + n) * 8, 8), 8), :] = jnp.where(low, folded[0], folded[1])
        return carry

    lax.fori_loop(0, LOCAL * SPECTRA // group, one, 0, unroll=UNROLL)
    for i in range(LOCAL):
        turned[pl.ds(i, 128, stride=LOCAL), :] = picked[i].T * (flags[i // 2].astype(jnp.float32) * (1.0 / math.sqrt(NCH)))
    values = turned[...].reshape(8, CAP, LOCAL, LANES).astype(jnp.bfloat16)
    out[0] = values
    out[1] = values


def channelize(voltages, filter_taps, station_flags, subband_lists):
    cos1, sin1 = table(FIRST, FIRST, FIRST)
    cos2, sin2 = table(SECOND, SECOND, SECOND)
    first_w = jnp.asarray(complex_block(cos1, sin1).T, jnp.bfloat16)
    second_w = jnp.asarray(complex_block(cos2, sin2), jnp.bfloat16)
    twid = jnp.asarray(np.stack(table(NCH, FIRST, SECOND)), jnp.float32)
    volts = voltages.reshape(2, LOCAL, SEGMENTS, NCH).transpose(0, 2, 1, 3)

    hbm = pl.BlockSpec(memory_space=pl.ANY)
    vmem = pl.BlockSpec(memory_space=pltpu.VMEM)
    return pl.pallas_call(
        channelize_kernel,
        in_specs=[hbm] * 5 + [vmem, pl.BlockSpec(memory_space=pltpu.SMEM)],
        out_specs=vmem,
        out_shape=jax.ShapeDtypeStruct((2, 8, CAP, LOCAL, LANES), jnp.bfloat16),
        scratch_shapes=[
            pltpu.VMEM((2, SPECTRA, LOCAL * PITCH, SECOND), jnp.float32),
            pltpu.VMEM((LOCAL, LANES, 128), jnp.float32),
            pltpu.VMEM((128 * LOCAL, LANES), jnp.float32),
            pltpu.VMEM((2 * FIRST, 2 * FIRST), jnp.bfloat16),
            pltpu.VMEM((2, FIRST, SECOND), jnp.float32),
            pltpu.VMEM((2 * SECOND, 2 * SECOND), jnp.bfloat16),
            pltpu.VMEM((2, SEGMENTS, LOCAL, NCH), jnp.bfloat16),
            pltpu.VMEM((TAPS, NCH), jnp.float32),
            pltpu.SemaphoreType.DMA((3,)),
            pltpu.SemaphoreType.DMA((len(CHUNKS), 2)),
        ],
        compiler_params=pltpu.CompilerParams(vmem_limit_bytes=VMEM_ALL),
        name="channelize",
    )(volts, filter_taps, first_w, twid, second_w, subband_lists, station_flags)


def correlate_kernel(count, *refs):
    places, counts, own = refs[:3]
    others = refs[3 : 3 + count]
    out, results, sems = refs[-3:]
    lane = lax.broadcasted_iota(jnp.int32, (64, LANES), 1)
    real_lane = lane // SUBW % 2 == 0
    zero = jnp.zeros((64, LANES), jnp.bfloat16)

    def one_slot(slot, carry):
        factor = jnp.where(slot < counts[places[0]], 1.0 / SPECTRA, 0.0)
        mine = own[:, slot].astype(jnp.float32).reshape(64, LANES) * factor
        crossed = jnp.where(real_lane, pltpu.roll(mine, LANES - SUBW, 1), -pltpu.roll(mine, SUBW, 1))
        left = jnp.concatenate(
            [
                jnp.concatenate(
                    [jnp.where(lane % SUBW == u, x, 0.0).astype(jnp.bfloat16) for x in (mine, crossed)], axis=1
                )
                for u in range(SUBW)
            ],
            axis=0,
        )
        rows = pl.ds(slot * SUBW, SUBW)
        for at in range(0, count, 2):
            right = []
            for n in range(at, min(at + 2, count)):
                block = others[n][:, slot].reshape(64, LANES)
                right += [jnp.concatenate([block, zero], axis=1), jnp.concatenate([zero, block], axis=1)]
            right = jnp.concatenate(right, axis=0)
            product = lax.dot_general(
                left, right, (((1,), (1,)), ((), ())), preferred_element_type=jnp.float32
            )
            for n in range(at, min(at + 2, count)):
                piece = product[:, (n - at) * 128 : (n - at + 1) * 128]
                results[n, rows] = piece.reshape(SUBW, 64, 128)
        for n in range(count):
            pltpu.make_async_copy(results.at[n, rows], out.at[places[n + 1], rows], sems.at[n]).start()
        return carry

    lax.fori_loop(0, CAP, one_slot, 0, unroll=CUNROLL)
    for n in range(count):
        pltpu.make_async_copy(results.at[n], out.at[places[n + 1]], sems.at[n]).wait()


CUNROLL = 4


def correlate(total, group, counts, own, pairs):
    places = jnp.stack([group] + [distance for distance, _ in pairs]).astype(jnp.int32)
    others = [block for _, block in pairs]
    count = len(others)
    args = [places, counts, own, *others]
    specs = [pl.BlockSpec(memory_space=pltpu.SMEM)] * 2 + [pl.BlockSpec(memory_space=pltpu.VMEM)] * (1 + count)
    aliases = {}
    if total is not None:
        aliases = {len(args): 0}
        args.append(total)
        specs.append(pl.BlockSpec(memory_space=pl.ANY))
    return pl.pallas_call(
        functools.partial(correlate_kernel, count),
        in_specs=specs,
        out_specs=pl.BlockSpec(memory_space=pl.ANY),
        out_shape=jax.ShapeDtypeStruct((9, CAP * SUBW, 64, 128), jnp.float32),
        scratch_shapes=[
            pltpu.VMEM((count, CAP * SUBW, 64, 128), jnp.float32),
            pltpu.SemaphoreType.DMA((count,)),
        ],
        input_output_aliases=aliases,
        compiler_params=pltpu.CompilerParams(vmem_limit_bytes=VMEM),
        name="correlate",
    )(*args)


def per_device(voltages, filter_taps, station_flags, subband_lists, subband_counts):
    stn = lax.axis_index("stn")
    row, col, core = stn // 8, stn // 2 % 4, stn % 2
    group = lax.axis_index("chan")

    selected = channelize(voltages, filter_taps, station_flags, subband_lists)
    selected = selected.reshape(16, CAP, LOCAL, LANES)
    members = [
        [(y * 8 + z * 2 + c) * 8 + g for y in range(2) for g in range(8)] for z in range(4) for c in range(2)
    ]
    rows = lax.all_to_all(selected, ("stn", "chan"), 0, 0, axis_index_groups=members, tiled=True)
    rows = rows.reshape(2, 8, CAP, LOCAL, LANES)

    def take(r):
        return lax.dynamic_index_in_dim(rows, r, 0, keepdims=False)

    def exchange(array, flip):
        return lax.ppermute(array, "stn", [(i, i ^ flip) for i in range(16)])

    own = take(row)
    far = take(1 - row)
    moved = {}
    for flip in (2, 1, 3):
        other = col ^ flip
        moved[flip] = exchange(jnp.where(col > other, own, far), flip * 2)
    spare = exchange(jnp.where(core == 0, far, own), 1)

    side = 1 - 2 * core
    ahead = {flip: 2 * ((col ^ flip) - col + 4) % 8 for flip in (1, 2, 3)}
    join = functools.partial(correlate, group=group, counts=subband_counts, own=own)
    total = join(None, pairs=[(0 * core, own), (0 * core + 8, far), (1 + 6 * core, spare)])
    *arrived, total = lax.optimization_barrier((*(moved[flip] for flip in (1, 3, 2)), total))
    pairs = []
    for flip, block in zip((1, 3, 2), arrived):
        pairs += [(ahead[flip], block), (ahead[flip] + side, exchange(block, 1))]
    total = join(total, pairs=pairs)
    return total[None]


def solution(mesh):
    placed = (P(None, ("stn", "chan"), None), P(), P(("stn", "chan")), P(), P())
    return jax.shard_map(
        per_device,
        mesh=mesh,
        in_specs=placed,
        out_specs=P("stn", None, "chan", None, None),
        check_vma=False,
    )
```

```python
import functools
import math

import jax
import jax.numpy as jnp
import numpy as np
from jax import lax
from jax.experimental import pallas as pl
from jax.experimental.pallas import tpu as pltpu
from jax.sharding import PartitionSpec as P

NCH = 8192
FIRST = 64
SECOND = 128
TAPS = 16
SPECTRA = 16
SUBW = 4
CAP = 16
SEGMENTS = SPECTRA + TAPS - 1
LOCAL = 8
LANES = SPECTRA * 2 * SUBW
CHUNKS = (256, 256, 512, 1024, 2048, 2048, 2048)
FUNROLL = 2
DIRECT = 4
PITCH = FIRST + 8
GROUP = 8
UNROLL = 8
VMEM = 48 * 1024 * 1024
VMEM_ALL = 60 * 1024 * 1024


def table(length, rows, cols):
    angles = (np.outer(np.arange(rows), np.arange(cols)) % length) * (2.0 * math.pi / length)
    return np.cos(angles), np.sin(angles)


def complex_block(cosine, sine):
    return np.block([[cosine, -sine], [sine, cosine]])


def split_taps(taps):
    half = len(taps) // 2
    if len(taps) <= DIRECT:
        return taps
    low, high = taps[:half], taps[half:]
    return split_taps(low), split_taps(high), split_taps([a + b for a, b in zip(low, high)])


def remembered(function):
    return functools.lru_cache(maxsize=None)(function)


def sliding(tree, length, value, emit, start=None):
    if isinstance(tree, list):
        totals = dict(enumerate(start or ()))
        for n in range(2 * length - 1):
            for j in range(length):
                t = n - j
                if 0 <= t < length:
                    term = tree[j] * value(n)
                    totals[t] = totals[t] + term if t in totals else term
            if n >= length - 1:
                emit(n - length + 1, totals.pop(n - length + 1))
        return
    low, high, both = tree
    half = length // 2
    shared = [None] * half
    sliding(both, half, lambda n: value(n + half), shared.__setitem__)
    first = shared if start is None else [a + b for a, b in zip(start[:half], shared)]
    sliding(low, half, remembered(lambda n: value(n) - value(n + half)), emit, first)
    second = shared if start is None else [a + b for a, b in zip(start[half:], shared)]
    late = remembered(lambda n: value(n + length) - value(n + half))
    sliding(high, half, late, lambda t, total: emit(t + half, total), second)


def channelize_kernel(*refs):
    volts_hbm, taps_hbm, first_hbm, twid_hbm, second_hbm, lists, flags, out = refs[:8]
    frames, picked, turned, first_w, twid, second_w, volts, taps, sems, fetched = refs[8:]

    copies = [
        pltpu.make_async_copy(source, target, sems.at[n])
        for n, (source, target) in enumerate(
            ((first_hbm, first_w), (twid_hbm, twid), (second_hbm, second_w))
        )
    ]

    starts = [sum(CHUNKS[:n]) for n in range(len(CHUNKS))]

    def pieces(n):
        lanes = pl.ds(starts[n], CHUNKS[n])
        return (
            pltpu.make_async_copy(taps_hbm.at[:, lanes], taps.at[:, lanes], fetched.at[n, 0]),
            pltpu.make_async_copy(
                volts_hbm.at[:, :, :, lanes], volts.at[:, :, :, lanes], fetched.at[n, 1]
            ),
        )

    for n in range(len(CHUNKS)):
        for copy in pieces(n):
            copy.start()
    for copy in copies:
        copy.start()

    def filter_one(at, carry):
        lanes = pl.ds(pl.multiple_of(at * SECOND, SECOND), SECOND)
        row = at
        coeffs = [jnp.broadcast_to(taps[j : j + 1, lanes], (LOCAL, SECOND)) for j in range(TAPS)]
        tree = split_taps(coeffs)
        for part in range(2):
            value = lambda seg: volts[part, seg, :, lanes].astype(jnp.float32)

            def store(t, total):
                frames[part, t, pl.ds(row, LOCAL, stride=PITCH), :] = total

            sliding(tree, TAPS, value, store)
        return carry

    for n in range(len(CHUNKS)):
        for copy in pieces(n):
            copy.wait()
        first_row = starts[n] // SECOND
        lax.fori_loop(first_row, first_row + CHUNKS[n] // SECOND, filter_one, 0, unroll=FUNROLL)

    for copy in copies:
        copy.wait()
    spread = lax.broadcasted_iota(jnp.int32, (CAP, 128), 1) % CAP == lax.broadcasted_iota(
        jnp.int32, (CAP, 128), 0
    )
    spread = spread.astype(jnp.bfloat16)
    diagonal = lax.broadcasted_iota(jnp.int32, (8, 128), 1) // CAP == lax.broadcasted_iota(
        jnp.int32, (8, 128), 0
    )

    def along_lanes(numbers):
        full = jnp.dot(numbers.astype(jnp.bfloat16), spread, preferred_element_type=jnp.float32)
        return jnp.sum(jnp.where(diagonal, full, 0.0), axis=0, keepdims=True).astype(jnp.int32)

    number_m = along_lanes(lists[...] // (FIRST // SUBW))
    number_k = along_lanes(lists[...] % (FIRST // SUBW))
    onehot = (lax.broadcasted_iota(jnp.int32, (SECOND, 128), 0) == number_m).astype(jnp.bfloat16)
    chosen = jnp.concatenate(
        [
            jnp.dot(second_w[:, q * SECOND : (q + 1) * SECOND], onehot, preferred_element_type=jnp.float32)
            for q in range(2)
        ],
        axis=1,
    ).astype(jnp.bfloat16)
    half = lax.broadcasted_iota(jnp.int32, (8, 128), 0) // SUBW
    masks = [number_k == 2 * v + half for v in range(FIRST // 8)]
    low = half == 0
    group = GROUP

    def one(index, carry):
        i = index // (SPECTRA // group)
        t0 = (index % (SPECTRA // group)) * group
        rows = pl.ds(pl.multiple_of(i * PITCH, 8), FIRST)
        block = jnp.concatenate(
            [
                jnp.concatenate([frames[part, t0 + n, rows, :] for part in range(2)], axis=0)
                for n in range(group)
            ],
            axis=1,
        ).astype(jnp.bfloat16)
        first = jnp.dot(first_w[...], block, preferred_element_type=jnp.float32)
        rotated = []
        for n in range(group):
            real = first[:FIRST, n * SECOND : (n + 1) * SECOND]
            imag = first[FIRST:, n * SECOND : (n + 1) * SECOND]
            cosine, sine = twid[0], twid[1]
            rotated.append(
                jnp.concatenate([real * cosine + imag * sine, imag * cosine - real * sine], axis=1)
            )
        rotated = jnp.concatenate(rotated, axis=0).astype(jnp.bfloat16)
        second = jnp.dot(rotated, chosen, preferred_element_type=jnp.float32)
        for n in range(group):
            folded = []
            for q in range(2):
                total = jnp.zeros((8, 128), jnp.float32)
                for v in range(FIRST // 8):
                    piece = second[n * FIRST + v * 8 : n * FIRST + v * 8 + 8, q * 128 : q * 128 + 128]
                    total = jnp.where(masks[v], piece, total)
                folded.append(total + pltpu.roll(total, SUBW, 0))
            picked[i, pl.ds(pl.multiple_of((t0 + n) * 8, 8), 8), :] = jnp.where(low, folded[0], folded[1])
        return carry

    lax.fori_loop(0, LOCAL * SPECTRA // group, one, 0, unroll=UNROLL)
    for i in range(LOCAL):
        turned[pl.ds(i, 128, stride=LOCAL), :] = picked[i].T * (flags[i // 2].astype(jnp.float32) * (1.0 / math.sqrt(NCH)))
    values = turned[...].reshape(8, CAP, LOCAL, LANES).astype(jnp.bfloat16)
    out[0] = values
    out[1] = values


def channelize(voltages, filter_taps, station_flags, subband_lists):
    cos1, sin1 = table(FIRST, FIRST, FIRST)
    cos2, sin2 = table(SECOND, SECOND, SECOND)
    first_w = jnp.asarray(complex_block(cos1, sin1).T, jnp.bfloat16)
    second_w = jnp.asarray(complex_block(cos2, sin2), jnp.bfloat16)
    twid = jnp.asarray(np.stack(table(NCH, FIRST, SECOND)), jnp.float32)
    volts = voltages.reshape(2, LOCAL, SEGMENTS, NCH).transpose(0, 2, 1, 3)

    hbm = pl.BlockSpec(memory_space=pl.ANY)
    vmem = pl.BlockSpec(memory_space=pltpu.VMEM)
    return pl.pallas_call(
        channelize_kernel,
        in_specs=[hbm] * 5 + [vmem, pl.BlockSpec(memory_space=pltpu.SMEM)],
        out_specs=vmem,
        out_shape=jax.ShapeDtypeStruct((2, 8, CAP, LOCAL, LANES), jnp.bfloat16),
        scratch_shapes=[
            pltpu.VMEM((2, SPECTRA, LOCAL * PITCH, SECOND), jnp.float32),
            pltpu.VMEM((LOCAL, LANES, 128), jnp.float32),
            pltpu.VMEM((128 * LOCAL, LANES), jnp.float32),
            pltpu.VMEM((2 * FIRST, 2 * FIRST), jnp.bfloat16),
            pltpu.VMEM((2, FIRST, SECOND), jnp.float32),
            pltpu.VMEM((2 * SECOND, 2 * SECOND), jnp.bfloat16),
            pltpu.VMEM((2, SEGMENTS, LOCAL, NCH), jnp.bfloat16),
            pltpu.VMEM((TAPS, NCH), jnp.float32),
            pltpu.SemaphoreType.DMA((3,)),
            pltpu.SemaphoreType.DMA((len(CHUNKS), 2)),
        ],
        compiler_params=pltpu.CompilerParams(vmem_limit_bytes=VMEM_ALL),
        name="channelize",
    )(volts, filter_taps, first_w, twid, second_w, subband_lists, station_flags)


def correlate_kernel(count, *refs):
    places, counts, own = refs[:3]
    others = refs[3 : 3 + count]
    out, results, sems = refs[-3:]
    lane = lax.broadcasted_iota(jnp.int32, (64, LANES), 1)
    real_lane = lane // SUBW % 2 == 0
    zero = jnp.zeros((64, LANES), jnp.bfloat16)

    def one_slot(slot, carry):
        factor = jnp.where(slot < counts[places[0]], 1.0 / SPECTRA, 0.0)
        mine = own[:, slot].astype(jnp.float32).reshape(64, LANES) * factor
        crossed = jnp.where(real_lane, pltpu.roll(mine, LANES - SUBW, 1), -pltpu.roll(mine, SUBW, 1))
        left = jnp.concatenate(
            [
                jnp.concatenate(
                    [jnp.where(lane % SUBW == u, x, 0.0).astype(jnp.bfloat16) for x in (mine, crossed)], axis=1
                )
                for u in range(SUBW)
            ],
            axis=0,
        )
        rows = pl.ds(slot * SUBW, SUBW)
        for at in range(0, count, 2):
            right = []
            for n in range(at, min(at + 2, count)):
                block = others[n][:, slot].reshape(64, LANES)
                right += [jnp.concatenate([block, zero], axis=1), jnp.concatenate([zero, block], axis=1)]
            right = jnp.concatenate(right, axis=0)
            product = lax.dot_general(
                left, right, (((1,), (1,)), ((), ())), preferred_element_type=jnp.float32
            )
            for n in range(at, min(at + 2, count)):
                piece = product[:, (n - at) * 128 : (n - at + 1) * 128]
                results[n, rows] = piece.reshape(SUBW, 64, 128)
        for n in range(count):
            pltpu.make_async_copy(results.at[n, rows], out.at[places[n + 1], rows], sems.at[n]).start()
        return carry

    lax.fori_loop(0, CAP, one_slot, 0, unroll=CUNROLL)
    for n in range(count):
        pltpu.make_async_copy(results.at[n], out.at[places[n + 1]], sems.at[n]).wait()


CUNROLL = 4


def correlate(total, group, counts, own, pairs):
    places = jnp.stack([group] + [distance for distance, _ in pairs]).astype(jnp.int32)
    others = [block for _, block in pairs]
    count = len(others)
    args = [places, counts, own, *others]
    specs = [pl.BlockSpec(memory_space=pltpu.SMEM)] * 2 + [pl.BlockSpec(memory_space=pltpu.VMEM)] * (1 + count)
    aliases = {}
    if total is not None:
        aliases = {len(args): 0}
        args.append(total)
        specs.append(pl.BlockSpec(memory_space=pl.ANY))
    return pl.pallas_call(
        functools.partial(correlate_kernel, count),
        in_specs=specs,
        out_specs=pl.BlockSpec(memory_space=pl.ANY),
        out_shape=jax.ShapeDtypeStruct((9, CAP * SUBW, 64, 128), jnp.float32),
        scratch_shapes=[
            pltpu.VMEM((count, CAP * SUBW, 64, 128), jnp.float32),
            pltpu.SemaphoreType.DMA((count,)),
        ],
        input_output_aliases=aliases,
        compiler_params=pltpu.CompilerParams(vmem_limit_bytes=VMEM),
        name="correlate",
    )(*args)


def per_device(voltages, filter_taps, station_flags, subband_lists, subband_counts):
    stn = lax.axis_index("stn")
    row, col, core = stn // 8, stn // 2 % 4, stn % 2
    group = lax.axis_index("chan")

    selected = channelize(voltages, filter_taps, station_flags, subband_lists)
    selected = selected.reshape(16, CAP, LOCAL, LANES)
    members = [
        [(y * 8 + z * 2 + c) * 8 + g for y in range(2) for g in range(8)] for z in range(4) for c in range(2)
    ]
    rows = lax.all_to_all(selected, ("stn", "chan"), 0, 0, axis_index_groups=members, tiled=True)
    rows = rows.reshape(2, 8, CAP, LOCAL, LANES)

    def take(r):
        return lax.dynamic_index_in_dim(rows, r, 0, keepdims=False)

    def exchange(array, flip):
        return lax.ppermute(array, "stn", [(i, i ^ flip) for i in range(16)])

    own = take(row)
    far = take(1 - row)
    moved = {}
    for flip in (2, 1, 3):
        other = col ^ flip
        moved[flip] = exchange(jnp.where(col > other, own, far), flip * 2)
    spare = exchange(jnp.where(core == 0, far, own), 1)

    side = 1 - 2 * core
    ahead = {flip: 2 * ((col ^ flip) - col + 4) % 8 for flip in (1, 2, 3)}
    join = functools.partial(correlate, group=group, counts=subband_counts, own=own)
    total = join(None, pairs=[(0 * core, own), (0 * core + 8, far), (1 + 6 * core, spare)])
    far_block, after = lax.optimization_barrier((moved[2], total))
    total = join(after, pairs=[(ahead[2], far_block)])
    *near, total = lax.optimization_barrier((moved[1], moved[3], total))
    pairs = [(ahead[2] + side, exchange(far_block, 1))]
    for flip, block in zip((1, 3), near):
        pairs += [(ahead[flip], block), (ahead[flip] + side, exchange(block, 1))]
    total = join(total, pairs=pairs)
    return total[None]


def solution(mesh):
    placed = (P(None, ("stn", "chan"), None), P(), P(("stn", "chan")), P(), P())
    return jax.shard_map(
        per_device,
        mesh=mesh,
        in_specs=placed,
        out_specs=P("stn", None, "chan", None, None),
        check_vma=False,
    )
```

```python
import functools
import math

import jax
import jax.numpy as jnp
import numpy as np
from jax import lax
from jax.experimental import pallas as pl
from jax.experimental.pallas import tpu as pltpu
from jax.sharding import PartitionSpec as P

NCH = 8192
FIRST = 64
SECOND = 128
TAPS = 16
SPECTRA = 16
SUBW = 4
CAP = 16
SEGMENTS = SPECTRA + TAPS - 1
LOCAL = 8
LANES = SPECTRA * 2 * SUBW
CHUNKS = (256, 256, 512, 1024, 2048, 2048, 2048)
FUNROLL = 2
DIRECT = 4
PITCH = FIRST + 8
GROUP = 16
UNROLL = 8
VMEM = 48 * 1024 * 1024
VMEM_ALL = 60 * 1024 * 1024


def table(length, rows, cols):
    angles = (np.outer(np.arange(rows), np.arange(cols)) % length) * (2.0 * math.pi / length)
    return np.cos(angles), np.sin(angles)


def complex_block(cosine, sine):
    return np.block([[cosine, -sine], [sine, cosine]])


def split_taps(taps):
    half = len(taps) // 2
    if len(taps) <= DIRECT:
        return taps
    low, high = taps[:half], taps[half:]
    return split_taps(low), split_taps(high), split_taps([a + b for a, b in zip(low, high)])


def remembered(function):
    return functools.lru_cache(maxsize=None)(function)


def sliding(tree, length, value, emit, start=None):
    if isinstance(tree, list):
        totals = dict(enumerate(start or ()))
        for n in range(2 * length - 1):
            for j in range(length):
                t = n - j
                if 0 <= t < length:
                    term = tree[j] * value(n)
                    totals[t] = totals[t] + term if t in totals else term
            if n >= length - 1:
                emit(n - length + 1, totals.pop(n - length + 1))
        return
    low, high, both = tree
    half = length // 2
    shared = [None] * half
    sliding(both, half, lambda n: value(n + half), shared.__setitem__)
    first = shared if start is None else [a + b for a, b in zip(start[:half], shared)]
    sliding(low, half, remembered(lambda n: value(n) - value(n + half)), emit, first)
    second = shared if start is None else [a + b for a, b in zip(start[half:], shared)]
    late = remembered(lambda n: value(n + length) - value(n + half))
    sliding(high, half, late, lambda t, total: emit(t + half, total), second)


def channelize_kernel(*refs):
    volts_hbm, taps_hbm, first_hbm, twid_hbm, second_hbm, lists, flags, out = refs[:8]
    frames, picked, turned, first_w, twid, second_w, volts, taps, sems, fetched = refs[8:]

    copies = [
        pltpu.make_async_copy(source, target, sems.at[n])
        for n, (source, target) in enumerate(
            ((first_hbm, first_w), (twid_hbm, twid), (second_hbm, second_w))
        )
    ]

    starts = [sum(CHUNKS[:n]) for n in range(len(CHUNKS))]

    def pieces(n):
        lanes = pl.ds(starts[n], CHUNKS[n])
        return (
            pltpu.make_async_copy(taps_hbm.at[:, lanes], taps.at[:, lanes], fetched.at[n, 0]),
            pltpu.make_async_copy(
                volts_hbm.at[:, :, :, lanes], volts.at[:, :, :, lanes], fetched.at[n, 1]
            ),
        )

    for n in range(len(CHUNKS)):
        for copy in pieces(n):
            copy.start()
    for copy in copies:
        copy.start()

    def filter_one(at, carry):
        lanes = pl.ds(pl.multiple_of(at * SECOND, SECOND), SECOND)
        row = at
        coeffs = [jnp.broadcast_to(taps[j : j + 1, lanes], (LOCAL, SECOND)) for j in range(TAPS)]
        tree = split_taps(coeffs)
        for part in range(2):
            value = lambda seg: volts[part, seg, :, lanes].astype(jnp.float32)

            def store(t, total):
                frames[part, t, pl.ds(row, LOCAL, stride=PITCH), :] = total

            sliding(tree, TAPS, value, store)
        return carry

    for n in range(len(CHUNKS)):
        for copy in pieces(n):
            copy.wait()
        first_row = starts[n] // SECOND
        lax.fori_loop(first_row, first_row + CHUNKS[n] // SECOND, filter_one, 0, unroll=FUNROLL)

    for copy in copies:
        copy.wait()
    spread = lax.broadcasted_iota(jnp.int32, (CAP, 128), 1) % CAP == lax.broadcasted_iota(
        jnp.int32, (CAP, 128), 0
    )
    spread = spread.astype(jnp.bfloat16)
    diagonal = lax.broadcasted_iota(jnp.int32, (8, 128), 1) // CAP == lax.broadcasted_iota(
        jnp.int32, (8, 128), 0
    )

    def along_lanes(numbers):
        full = jnp.dot(numbers.astype(jnp.bfloat16), spread, preferred_element_type=jnp.float32)
        return jnp.sum(jnp.where(diagonal, full, 0.0), axis=0, keepdims=True).astype(jnp.int32)

    number_m = along_lanes(lists[...] // (FIRST // SUBW))
    number_k = along_lanes(lists[...] % (FIRST // SUBW))
    onehot = (lax.broadcasted_iota(jnp.int32, (SECOND, 128), 0) == number_m).astype(jnp.bfloat16)
    chosen = jnp.concatenate(
        [
            jnp.dot(second_w[:, q * SECOND : (q + 1) * SECOND], onehot, preferred_element_type=jnp.float32)
            for q in range(2)
        ],
        axis=1,
    ).astype(jnp.bfloat16)
    half = lax.broadcasted_iota(jnp.int32, (8, 128), 0) // SUBW
    masks = [number_k == 2 * v + half for v in range(FIRST // 8)]
    low = half == 0
    group = GROUP

    def one(index, carry):
        i = index // (SPECTRA // group)
        t0 = (index % (SPECTRA // group)) * group
        rows = pl.ds(pl.multiple_of(i * PITCH, 8), FIRST)
        block = jnp.concatenate(
            [
                jnp.concatenate([frames[part, t0 + n, rows, :] for part in range(2)], axis=0)
                for n in range(group)
            ],
            axis=1,
        ).astype(jnp.bfloat16)
        first = jnp.dot(first_w[...], block, preferred_element_type=jnp.float32)
        rotated = []
        for n in range(group):
            real = first[:FIRST, n * SECOND : (n + 1) * SECOND]
            imag = first[FIRST:, n * SECOND : (n + 1) * SECOND]
            cosine, sine = twid[0], twid[1]
            rotated.append(
                jnp.concatenate([real * cosine + imag * sine, imag * cosine - real * sine], axis=1)
            )
        rotated = jnp.concatenate(rotated, axis=0).astype(jnp.bfloat16)
        second = jnp.dot(rotated, chosen, preferred_element_type=jnp.float32)
        for n in range(group):
            folded = []
            for q in range(2):
                total = jnp.zeros((8, 128), jnp.float32)
                for v in range(FIRST // 8):
                    piece = second[n * FIRST + v * 8 : n * FIRST + v * 8 + 8, q * 128 : q * 128 + 128]
                    total = jnp.where(masks[v], piece, total)
                folded.append(total + pltpu.roll(total, SUBW, 0))
            picked[i, pl.ds(pl.multiple_of((t0 + n) * 8, 8), 8), :] = jnp.where(low, folded[0], folded[1])
        return carry

    lax.fori_loop(0, LOCAL * SPECTRA // group, one, 0, unroll=UNROLL)
    for i in range(LOCAL):
        turned[pl.ds(i, 128, stride=LOCAL), :] = picked[i].T * (flags[i // 2].astype(jnp.float32) * (1.0 / math.sqrt(NCH)))
    values = turned[...].reshape(8, CAP, LOCAL, LANES).astype(jnp.bfloat16)
    out[0] = values
    out[1] = values


def channelize(voltages, filter_taps, station_flags, subband_lists):
    cos1, sin1 = table(FIRST, FIRST, FIRST)
    cos2, sin2 = table(SECOND, SECOND, SECOND)
    first_w = jnp.asarray(complex_block(cos1, sin1).T, jnp.bfloat16)
    second_w = jnp.asarray(complex_block(cos2, sin2), jnp.bfloat16)
    twid = jnp.asarray(np.stack(table(NCH, FIRST, SECOND)), jnp.float32)
    volts = voltages.reshape(2, LOCAL, SEGMENTS, NCH).transpose(0, 2, 1, 3)

    hbm = pl.BlockSpec(memory_space=pl.ANY)
    vmem = pl.BlockSpec(memory_space=pltpu.VMEM)
    return pl.pallas_call(
        channelize_kernel,
        in_specs=[hbm] * 5 + [vmem, pl.BlockSpec(memory_space=pltpu.SMEM)],
        out_specs=vmem,
        out_shape=jax.ShapeDtypeStruct((2, 8, CAP, LOCAL, LANES), jnp.bfloat16),
        scratch_shapes=[
            pltpu.VMEM((2, SPECTRA, LOCAL * PITCH, SECOND), jnp.float32),
            pltpu.VMEM((LOCAL, LANES, 128), jnp.float32),
            pltpu.VMEM((128 * LOCAL, LANES), jnp.float32),
            pltpu.VMEM((2 * FIRST, 2 * FIRST), jnp.bfloat16),
            pltpu.VMEM((2, FIRST, SECOND), jnp.float32),
            pltpu.VMEM((2 * SECOND, 2 * SECOND), jnp.bfloat16),
            pltpu.VMEM((2, SEGMENTS, LOCAL, NCH), jnp.bfloat16),
            pltpu.VMEM((TAPS, NCH), jnp.float32),
            pltpu.SemaphoreType.DMA((3,)),
            pltpu.SemaphoreType.DMA((len(CHUNKS), 2)),
        ],
        compiler_params=pltpu.CompilerParams(vmem_limit_bytes=VMEM_ALL),
        name="channelize",
    )(volts, filter_taps, first_w, twid, second_w, subband_lists, station_flags)


def correlate_kernel(count, *refs):
    places, counts, own = refs[:3]
    others = refs[3 : 3 + count]
    out, results, sems = refs[-3:]
    lane = lax.broadcasted_iota(jnp.int32, (64, LANES), 1)
    real_lane = lane // SUBW % 2 == 0
    zero = jnp.zeros((64, LANES), jnp.bfloat16)

    def one_slot(slot, carry):
        factor = jnp.where(slot < counts[places[0]], 1.0 / SPECTRA, 0.0)
        mine = own[:, slot].astype(jnp.float32).reshape(64, LANES) * factor
        crossed = jnp.where(real_lane, pltpu.roll(mine, LANES - SUBW, 1), -pltpu.roll(mine, SUBW, 1))
        left = jnp.concatenate(
            [
                jnp.concatenate(
                    [jnp.where(lane % SUBW == u, x, 0.0).astype(jnp.bfloat16) for x in (mine, crossed)], axis=1
                )
                for u in range(SUBW)
            ],
            axis=0,
        )
        rows = pl.ds(slot * SUBW, SUBW)
        for at in range(0, count, 2):
            right = []
            for n in range(at, min(at + 2, count)):
                block = others[n][:, slot].reshape(64, LANES)
                right += [jnp.concatenate([block, zero], axis=1), jnp.concatenate([zero, block], axis=1)]
            right = jnp.concatenate(right, axis=0)
            product = lax.dot_general(
                left, right, (((1,), (1,)), ((), ())), preferred_element_type=jnp.float32
            )
            for n in range(at, min(at + 2, count)):
                piece = product[:, (n - at) * 128 : (n - at + 1) * 128]
                results[n, rows] = piece.reshape(SUBW, 64, 128)
        for n in range(count):
            pltpu.make_async_copy(results.at[n, rows], out.at[places[n + 1], rows], sems.at[n]).start()
        return carry

    lax.fori_loop(0, CAP, one_slot, 0, unroll=CUNROLL)
    for n in range(count):
        pltpu.make_async_copy(results.at[n], out.at[places[n + 1]], sems.at[n]).wait()


CUNROLL = 4


def correlate(total, group, counts, own, pairs):
    places = jnp.stack([group] + [distance for distance, _ in pairs]).astype(jnp.int32)
    others = [block for _, block in pairs]
    count = len(others)
    args = [places, counts, own, *others]
    specs = [pl.BlockSpec(memory_space=pltpu.SMEM)] * 2 + [pl.BlockSpec(memory_space=pltpu.VMEM)] * (1 + count)
    aliases = {}
    if total is not None:
        aliases = {len(args): 0}
        args.append(total)
        specs.append(pl.BlockSpec(memory_space=pl.ANY))
    return pl.pallas_call(
        functools.partial(correlate_kernel, count),
        in_specs=specs,
        out_specs=pl.BlockSpec(memory_space=pl.ANY),
        out_shape=jax.ShapeDtypeStruct((9, CAP * SUBW, 64, 128), jnp.float32),
        scratch_shapes=[
            pltpu.VMEM((count, CAP * SUBW, 64, 128), jnp.float32),
            pltpu.SemaphoreType.DMA((count,)),
        ],
        input_output_aliases=aliases,
        compiler_params=pltpu.CompilerParams(vmem_limit_bytes=VMEM),
        name="correlate",
    )(*args)


def per_device(voltages, filter_taps, station_flags, subband_lists, subband_counts):
    stn = lax.axis_index("stn")
    row, col, core = stn // 8, stn // 2 % 4, stn % 2
    group = lax.axis_index("chan")

    selected = channelize(voltages, filter_taps, station_flags, subband_lists)
    selected = selected.reshape(16, CAP, LOCAL, LANES)
    members = [
        [(y * 8 + z * 2 + c) * 8 + g for y in range(2) for g in range(8)] for z in range(4) for c in range(2)
    ]
    rows = lax.all_to_all(selected, ("stn", "chan"), 0, 0, axis_index_groups=members, tiled=True)
    rows = rows.reshape(2, 8, CAP, LOCAL, LANES)

    def take(r):
        return lax.dynamic_index_in_dim(rows, r, 0, keepdims=False)

    def exchange(array, flip):
        return lax.ppermute(array, "stn", [(i, i ^ flip) for i in range(16)])

    own = take(row)
    far = take(1 - row)
    moved = {}
    for flip in (2, 1, 3):
        other = col ^ flip
        moved[flip] = exchange(jnp.where(col > other, own, far), flip * 2)
    spare = exchange(jnp.where(core == 0, far, own), 1)

    side = 1 - 2 * core
    ahead = {flip: 2 * ((col ^ flip) - col + 4) % 8 for flip in (1, 2, 3)}
    join = functools.partial(correlate, group=group, counts=subband_counts, own=own)
    total = join(None, pairs=[(0 * core, own), (0 * core + 8, far), (1 + 6 * core, spare)])
    far_block, after = lax.optimization_barrier((moved[2], total))
    total = join(after, pairs=[(ahead[2], far_block)])
    *near, total = lax.optimization_barrier((moved[1], moved[3], total))
    pairs = [(ahead[2] + side, exchange(far_block, 1))]
    for flip, block in zip((1, 3), near):
        pairs += [(ahead[flip], block), (ahead[flip] + side, exchange(block, 1))]
    total = join(total, pairs=pairs)
    return total[None]


def solution(mesh):
    placed = (P(None, ("stn", "chan"), None), P(), P(("stn", "chan")), P(), P())
    return jax.shard_map(
        per_device,
        mesh=mesh,
        in_specs=placed,
        out_specs=P("stn", None, "chan", None, None),
        check_vma=False,
    )
```

```python
import functools
import math

import jax
import jax.numpy as jnp
import numpy as np
from jax import lax
from jax.experimental import pallas as pl
from jax.experimental.pallas import tpu as pltpu
from jax.sharding import PartitionSpec as P

NCH = 8192
FIRST = 64
SECOND = 128
TAPS = 16
SPECTRA = 16
SUBW = 4
CAP = 16
SEGMENTS = SPECTRA + TAPS - 1
LOCAL = 8
LANES = SPECTRA * 2 * SUBW
CHUNKS = (256, 256, 512, 1024, 2048, 2048, 2048)
FUNROLL = 2
DIRECT = 4
PITCH = FIRST + 8
GROUP = 16
UNROLL = 8
VMEM = 48 * 1024 * 1024
VMEM_ALL = 60 * 1024 * 1024


def table(length, rows, cols):
    angles = (np.outer(np.arange(rows), np.arange(cols)) % length) * (2.0 * math.pi / length)
    return np.cos(angles), np.sin(angles)


def complex_block(cosine, sine):
    return np.block([[cosine, -sine], [sine, cosine]])


def split_taps(taps):
    half = len(taps) // 2
    if len(taps) <= DIRECT:
        return taps
    low, high = taps[:half], taps[half:]
    return split_taps(low), split_taps(high), split_taps([a + b for a, b in zip(low, high)])


def remembered(function):
    return functools.lru_cache(maxsize=None)(function)


def sliding(tree, length, value, emit, start=None):
    if isinstance(tree, list):
        totals = dict(enumerate(start or ()))
        for n in range(2 * length - 1):
            for j in range(length):
                t = n - j
                if 0 <= t < length:
                    term = tree[j] * value(n)
                    totals[t] = totals[t] + term if t in totals else term
            if n >= length - 1:
                emit(n - length + 1, totals.pop(n - length + 1))
        return
    low, high, both = tree
    half = length // 2
    shared = [None] * half
    sliding(both, half, lambda n: value(n + half), shared.__setitem__)
    first = shared if start is None else [a + b for a, b in zip(start[:half], shared)]
    sliding(low, half, remembered(lambda n: value(n) - value(n + half)), emit, first)
    second = shared if start is None else [a + b for a, b in zip(start[half:], shared)]
    late = remembered(lambda n: value(n + length) - value(n + half))
    sliding(high, half, late, lambda t, total: emit(t + half, total), second)


def channelize_kernel(*refs):
    volts_hbm, taps_hbm, first_hbm, twid_hbm, second_hbm, lists, flags, out = refs[:8]
    frames, picked, turned, first_w, twid, second_w, volts, taps, sems, fetched = refs[8:]

    copies = [
        pltpu.make_async_copy(source, target, sems.at[n])
        for n, (source, target) in enumerate(
            ((first_hbm, first_w), (twid_hbm, twid), (second_hbm, second_w))
        )
    ]

    starts = [sum(CHUNKS[:n]) for n in range(len(CHUNKS))]

    def pieces(n):
        lanes = pl.ds(starts[n], CHUNKS[n])
        return (
            pltpu.make_async_copy(taps_hbm.at[:, lanes], taps.at[:, lanes], fetched.at[n, 0]),
            pltpu.make_async_copy(
                volts_hbm.at[:, :, :, lanes], volts.at[:, :, :, lanes], fetched.at[n, 1]
            ),
        )

    for n in range(len(CHUNKS)):
        for copy in pieces(n):
            copy.start()
    for copy in copies:
        copy.start()

    def filter_one(at, carry):
        lanes = pl.ds(pl.multiple_of(at * SECOND, SECOND), SECOND)
        row = at
        coeffs = [jnp.broadcast_to(taps[j : j + 1, lanes], (LOCAL, SECOND)) for j in range(TAPS)]
        tree = split_taps(coeffs)
        for part in range(2):
            value = lambda seg: volts[part, seg, :, lanes].astype(jnp.float32)

            def store(t, total):
                frames[part, t, pl.ds(row, LOCAL, stride=PITCH), :] = total

            sliding(tree, TAPS, value, store)
        return carry

    for n in range(len(CHUNKS)):
        for copy in pieces(n):
            copy.wait()
        first_row = starts[n] // SECOND
        lax.fori_loop(first_row, first_row + CHUNKS[n] // SECOND, filter_one, 0, unroll=FUNROLL)

    for copy in copies:
        copy.wait()
    spread = lax.broadcasted_iota(jnp.int32, (CAP, 128), 1) % CAP == lax.broadcasted_iota(
        jnp.int32, (CAP, 128), 0
    )
    spread = spread.astype(jnp.bfloat16)
    diagonal = lax.broadcasted_iota(jnp.int32, (8, 128), 1) // CAP == lax.broadcasted_iota(
        jnp.int32, (8, 128), 0
    )

    def along_lanes(numbers):
        full = jnp.dot(numbers.astype(jnp.bfloat16), spread, preferred_element_type=jnp.float32)
        return jnp.sum(jnp.where(diagonal, full, 0.0), axis=0, keepdims=True).astype(jnp.int32)

    number_m = along_lanes(lists[...] // (FIRST // SUBW))
    number_k = along_lanes(lists[...] % (FIRST // SUBW))
    onehot = (lax.broadcasted_iota(jnp.int32, (SECOND, 128), 0) == number_m).astype(jnp.bfloat16)
    chosen = jnp.concatenate(
        [
            jnp.dot(second_w[:, q * SECOND : (q + 1) * SECOND], onehot, preferred_element_type=jnp.float32)
            for q in range(2)
        ],
        axis=1,
    ).astype(jnp.bfloat16)
    half = lax.broadcasted_iota(jnp.int32, (8, 128), 0) // SUBW
    masks = [number_k == 2 * v + half for v in range(FIRST // 8)]
    low = half == 0
    group = GROUP

    def one(index, carry):
        i = index // (SPECTRA // group)
        t0 = (index % (SPECTRA // group)) * group
        rows = pl.ds(pl.multiple_of(i * PITCH, 8), FIRST)
        block = jnp.concatenate(
            [
                jnp.concatenate([frames[part, t0 + n, rows, :] for part in range(2)], axis=0)
                for n in range(group)
            ],
            axis=1,
        ).astype(jnp.bfloat16)
        first = jnp.dot(first_w[...], block, preferred_element_type=jnp.float32)
        rotated = []
        for n in range(group):
            real = first[:FIRST, n * SECOND : (n + 1) * SECOND]
            imag = first[FIRST:, n * SECOND : (n + 1) * SECOND]
            cosine, sine = twid[0], twid[1]
            rotated.append(
                jnp.concatenate([real * cosine + imag * sine, imag * cosine - real * sine], axis=1)
            )
        rotated = jnp.concatenate(rotated, axis=0).astype(jnp.bfloat16)
        second = jnp.dot(rotated, chosen, preferred_element_type=jnp.float32)
        for n in range(group):
            folded = []
            for q in range(2):
                total = jnp.zeros((8, 128), jnp.float32)
                for v in range(FIRST // 8):
                    piece = second[n * FIRST + v * 8 : n * FIRST + v * 8 + 8, q * 128 : q * 128 + 128]
                    total = jnp.where(masks[v], piece, total)
                folded.append(total + pltpu.roll(total, SUBW, 0))
            picked[i, pl.ds(pl.multiple_of((t0 + n) * 8, 8), 8), :] = jnp.where(low, folded[0], folded[1])
        return carry

    lax.fori_loop(0, LOCAL * SPECTRA // group, one, 0, unroll=UNROLL)
    for i in range(LOCAL):
        turned[pl.ds(i, 128, stride=LOCAL), :] = picked[i].T * (flags[i // 2].astype(jnp.float32) * (1.0 / math.sqrt(NCH)))
    values = turned[...].reshape(8, CAP, LOCAL, LANES).astype(jnp.bfloat16)
    out[0] = values
    out[1] = values


def channelize(voltages, filter_taps, station_flags, subband_lists):
    cos1, sin1 = table(FIRST, FIRST, FIRST)
    cos2, sin2 = table(SECOND, SECOND, SECOND)
    first_w = jnp.asarray(complex_block(cos1, sin1).T, jnp.bfloat16)
    second_w = jnp.asarray(complex_block(cos2, sin2), jnp.bfloat16)
    twid = jnp.asarray(np.stack(table(NCH, FIRST, SECOND)), jnp.float32)
    volts = voltages.reshape(2, LOCAL, SEGMENTS, NCH).transpose(0, 2, 1, 3)

    hbm = pl.BlockSpec(memory_space=pl.ANY)
    vmem = pl.BlockSpec(memory_space=pltpu.VMEM)
    return pl.pallas_call(
        channelize_kernel,
        in_specs=[hbm] * 5 + [vmem, pl.BlockSpec(memory_space=pltpu.SMEM)],
        out_specs=vmem,
        out_shape=jax.ShapeDtypeStruct((2, 8, CAP, LOCAL, LANES), jnp.bfloat16),
        scratch_shapes=[
            pltpu.VMEM((2, SPECTRA, LOCAL * PITCH, SECOND), jnp.float32),
            pltpu.VMEM((LOCAL, LANES, 128), jnp.float32),
            pltpu.VMEM((128 * LOCAL, LANES), jnp.float32),
            pltpu.VMEM((2 * FIRST, 2 * FIRST), jnp.bfloat16),
            pltpu.VMEM((2, FIRST, SECOND), jnp.float32),
            pltpu.VMEM((2 * SECOND, 2 * SECOND), jnp.bfloat16),
            pltpu.VMEM((2, SEGMENTS, LOCAL, NCH), jnp.bfloat16),
            pltpu.VMEM((TAPS, NCH), jnp.float32),
            pltpu.SemaphoreType.DMA((3,)),
            pltpu.SemaphoreType.DMA((len(CHUNKS), 2)),
        ],
        compiler_params=pltpu.CompilerParams(vmem_limit_bytes=VMEM_ALL),
        name="channelize",
    )(volts, filter_taps, first_w, twid, second_w, subband_lists, station_flags)


def correlate_kernel(count, *refs):
    places, counts, own = refs[:3]
    others = refs[3 : 3 + count]
    out, results, sems = refs[-3:]
    lane = lax.broadcasted_iota(jnp.int32, (64, LANES), 1)
    real_lane = lane // SUBW % 2 == 0
    zero = jnp.zeros((64, LANES), jnp.bfloat16)

    def one_slot(slot, carry):
        factor = jnp.where(slot < counts[places[0]], 1.0 / SPECTRA, 0.0)
        mine = own[:, slot].astype(jnp.float32).reshape(64, LANES) * factor
        crossed = jnp.where(real_lane, pltpu.roll(mine, LANES - SUBW, 1), -pltpu.roll(mine, SUBW, 1))
        left = jnp.concatenate(
            [
                jnp.concatenate(
                    [jnp.where(lane % SUBW == u, x, 0.0).astype(jnp.bfloat16) for x in (mine, crossed)], axis=1
                )
                for u in range(SUBW)
            ],
            axis=0,
        )
        rows = pl.ds(slot * SUBW, SUBW)
        for at in range(0, count, 2):
            right = []
            for n in range(at, min(at + 2, count)):
                block = others[n][:, slot].reshape(64, LANES)
                right += [jnp.concatenate([block, zero], axis=1), jnp.concatenate([zero, block], axis=1)]
            right = jnp.concatenate(right, axis=0)
            product = lax.dot_general(
                left, right, (((1,), (1,)), ((), ())), preferred_element_type=jnp.float32
            )
            for n in range(at, min(at + 2, count)):
                piece = product[:, (n - at) * 128 : (n - at + 1) * 128]
                results[n, rows] = piece.reshape(SUBW, 64, 128)
        for n in range(count):
            pltpu.make_async_copy(results.at[n, rows], out.at[places[n + 1], rows], sems.at[n]).start()
        return carry

    lax.fori_loop(0, CAP, one_slot, 0, unroll=CUNROLL)
    for n in range(count):
        pltpu.make_async_copy(results.at[n], out.at[places[n + 1]], sems.at[n]).wait()


CUNROLL = 4


def correlate(total, group, counts, own, pairs):
    places = jnp.stack([group] + [distance for distance, _ in pairs]).astype(jnp.int32)
    others = [block for _, block in pairs]
    count = len(others)
    args = [places, counts, own, *others]
    specs = [pl.BlockSpec(memory_space=pltpu.SMEM)] * 2 + [pl.BlockSpec(memory_space=pltpu.VMEM)] * (1 + count)
    aliases = {}
    if total is not None:
        aliases = {len(args): 0}
        args.append(total)
        specs.append(pl.BlockSpec(memory_space=pl.ANY))
    return pl.pallas_call(
        functools.partial(correlate_kernel, count),
        in_specs=specs,
        out_specs=pl.BlockSpec(memory_space=pl.ANY),
        out_shape=jax.ShapeDtypeStruct((9, CAP * SUBW, 64, 128), jnp.float32),
        scratch_shapes=[
            pltpu.VMEM((count, CAP * SUBW, 64, 128), jnp.float32),
            pltpu.SemaphoreType.DMA((count,)),
        ],
        input_output_aliases=aliases,
        compiler_params=pltpu.CompilerParams(vmem_limit_bytes=VMEM),
        name="correlate",
    )(*args)


def per_device(voltages, filter_taps, station_flags, subband_lists, subband_counts):
    stn = lax.axis_index("stn")
    row, col, core = stn // 8, stn // 2 % 4, stn % 2
    group = lax.axis_index("chan")

    selected = channelize(voltages, filter_taps, station_flags, subband_lists)
    selected = selected.reshape(16, CAP, LOCAL, LANES)
    members = [
        [(y * 8 + z * 2 + c) * 8 + g for y in range(2) for g in range(8)] for z in range(4) for c in range(2)
    ]
    rows = lax.all_to_all(selected, ("stn", "chan"), 0, 0, axis_index_groups=members, tiled=True)
    rows = rows.reshape(2, 8, CAP, LOCAL, LANES)

    def take(r):
        return lax.dynamic_index_in_dim(rows, r, 0, keepdims=False)

    def exchange(array, flip):
        return lax.ppermute(array, "stn", [(i, i ^ flip) for i in range(16)])

    own = take(row)
    far = take(1 - row)
    moved = {}
    for flip in (2, 1, 3):
        other = col ^ flip
        moved[flip] = exchange(jnp.where(col > other, own, far), flip * 2)
    spare = exchange(jnp.where(core == 0, far, own), 1)

    side = 1 - 2 * core
    ahead = {flip: 2 * ((col ^ flip) - col + 4) % 8 for flip in (1, 2, 3)}
    join = functools.partial(correlate, group=group, counts=subband_counts, own=own)
    total = join(None, pairs=[(0 * core, own), (0 * core + 8, far), (1 + 6 * core, spare)])
    far_block, after = lax.optimization_barrier((moved[2], total))
    total = join(after, pairs=[(ahead[2], far_block)])
    passed = exchange(far_block, 1)
    *near, passed, total = lax.optimization_barrier((moved[1], moved[3], passed, total))
    pairs = [(ahead[2] + side, passed)]
    for flip, block in zip((1, 3), near):
        pairs += [(ahead[flip], block), (ahead[flip] + side, exchange(block, 1))]
    total = join(total, pairs=pairs)
    return total[None]


def solution(mesh):
    placed = (P(None, ("stn", "chan"), None), P(), P(("stn", "chan")), P(), P())
    return jax.shard_map(
        per_device,
        mesh=mesh,
        in_specs=placed,
        out_specs=P("stn", None, "chan", None, None),
        check_vma=False,
    )
```
